32 devices in a mesh: rows: 4 (over z), cols: 8 (over y, x, core).
Axes of the slice: x: 2, y: 2, z: 4, core: 2. Of those that a mesh axis runs over, the one named last changes fastest.
Arguments:
- density: bfloat16 [6144, 6144], P('rows', 'cols')
- points: float32 [1536, 3, 256], P(('rows', 'cols')), may hold values from -1 to 1
- grid_weights: float32 [1536, 256], P(('rows', 'cols')), may hold values from 0.002 to 0.02
- centres: float32 [3, 6144], replicated, may hold values from -1 to 1
- exponents: float32 [6144], replicated, may hold values from 3 to 12
- sig_blocks: int32 [1536, 4], P(('rows', 'cols')), may hold values from 0 to 47, as said below
- live_count: int32 [32], P(('rows', 'cols')), may hold values from 1 to 48, as said below
Outputs:
- xc_diag: float32 [6144, 1536], P('rows', 'cols')
- batch_energy: float32 [1536], P(('rows', 'cols'))
- exc_total: float32 [], replicated
The draws below stay inside these ranges and needn't reach their ends.
Inputs may be any that keep to these rules, and one draw needn't show every extreme that they name: `sig_blocks`: each row holds 4 different blocks in rising order, all among the 48 // 4 blocks of the batch's row group. `live_count`: some device has all 48 slots in use.
All inputs are finite; a program needn't handle non-finite values.
Results may differ from the reference program's by a relative error of at most 0.0005.
Values may be sent and summed in bfloat16 or wider, within the bound.
A program may use at most 64 MiB of HBM per device.

```python
import math
import jax
import jax.numpy as jnp
from jax import lax

BLOCK = 128
NBLK = 48
NSIG = 4
PTS = 256
BAT_DEV = 48
NBASIS = 6144
BATCHES = 1536
N_ROWS = 4
N_COLS = 8
DEVICES = 32


def draw_density(key, part):
    first, second = jax.random.split(jax.random.fold_in(key, 11), 2)
    scale = 40.0 / (NSIG * BLOCK)
    spread = 1.2 * scale
    raw = jnp.clip(jax.random.normal(first, (NBASIS, NBASIS), jnp.float32), -4.0, 4.0)
    diag = jax.random.uniform(second, (NBASIS,), jnp.float32, 1.0, 3.0)
    sym = (raw + raw.T) * (spread * 0.70710678)
    sym = sym - jnp.diag(jnp.diag(sym))
    full = sym + jnp.diag(diag * scale)
    return full.astype(jnp.bfloat16)


def draw_sig_blocks(key, part):
    span = NBLK // N_ROWS
    scores = jax.random.randint(jax.random.fold_in(key, 23), (BATCHES, span), 0, 1 << 20)
    scores = scores * span + jnp.arange(span, dtype=jnp.int32)[None, :]
    chosen = jnp.sort(jnp.argsort(scores, axis=1)[:, :NSIG].astype(jnp.int32), axis=1)
    group = (jnp.arange(BATCHES, dtype=jnp.int32) // (BAT_DEV * N_COLS))[:, None]
    return (chosen + group * span).astype(jnp.int32)


def draw_live_count(key, part):
    first, second = jax.random.split(jax.random.fold_in(key, 37))
    counts = jax.random.randint(first, (DEVICES,), 1, BAT_DEV + 1)
    full = jax.random.randint(second, (), 0, DEVICES)
    return jnp.where(jnp.arange(DEVICES) == full, BAT_DEV, counts).astype(jnp.int32)


def shard_levels(key, dims, pieces, low, high):
    factor_of, own = 1.0, jax.random.fold_in(key, 6)
    for position, parts in pieces:
        heights = jnp.exp(jax.random.uniform(jax.random.fold_in(own, position), (parts,), jnp.float32, low / len(pieces), high / len(pieces)))
        factor_of = factor_of * jnp.repeat(heights, dims[position] // parts).reshape([-1 if axis == position else 1 for axis in range(len(dims))])
    return factor_of


def setup_inputs(seed: int = 0) -> dict:
    seeds = jax.random.split(jax.random.key(seed), 8)
    density = draw_density(jax.random.fold_in(seeds[7], 71), 0)
    points = jnp.clip(jax.random.uniform(seeds[1], (BATCHES, 3, PTS), jnp.float32, -1.0, 1.0) * shard_levels(seeds[1], (BATCHES, 3, PTS), ((0, 32),), -0.4, 0.0), -1.0, 1.0)
    grid_weights = jnp.clip(jnp.exp(math.log(0.02) - 2.30258502 * jax.random.uniform(seeds[2], (BATCHES, PTS), jnp.float32) ** shard_levels(seeds[2], (BATCHES, PTS), ((0, 32),), -0.2, 0.2)), 0.002, 0.02)
    centres = jnp.clip(jax.random.uniform(seeds[3], (3, NBASIS), jnp.float32, -1.0, 1.0), -1.0, 1.0)
    exponents = jnp.clip(jnp.exp(jax.random.uniform(seeds[4], (NBASIS,), jnp.float32, math.log(3.0), math.log(12.0))), 3.0, 12.0)
    sig_blocks = draw_sig_blocks(jax.random.fold_in(seeds[7], 71), 0)
    live_count = draw_live_count(jax.random.fold_in(seeds[7], 71), 0)
    return {"density": density, "points": points, "grid_weights": grid_weights, "centres": centres, "exponents": exponents, "sig_blocks": sig_blocks, "live_count": live_count}


slater = 0.7386


def evaluate(coords, centre_sel, expo_sel):
    gap_x = coords[0][None, :] - centre_sel[0][:, None]
    gap_y = coords[1][None, :] - centre_sel[1][:, None]
    gap_z = coords[2][None, :] - centre_sel[2][:, None]
    dist = gap_x * gap_x + gap_y * gap_y + gap_z * gap_z
    return jnp.exp(-expo_sel[:, None] * dist).astype(jnp.bfloat16)


def reference(density, points, grid_weights, centres, exponents, sig_blocks, live_count):
    span = NBLK // N_ROWS
    dens4 = density.reshape(NBLK, BLOCK, NBLK, BLOCK)
    width = NSIG * BLOCK
    centre3 = centres.reshape(3, NBLK, BLOCK)
    expo2 = exponents.reshape(NBLK, BLOCK)

    def step(carry, item):
        coords, weight, sig, index = item
        group = index // (BAT_DEV * N_COLS)
        live = ((index % BAT_DEV) < live_count[index // BAT_DEV]).astype(jnp.float32)
        centre_sel = jnp.take(centre3, sig, axis=1).reshape(3, width)
        expo_sel = jnp.take(expo2, sig, axis=0).reshape(width)
        phi = evaluate(coords, centre_sel, expo_sel)
        p_ss = jnp.take(jnp.take(dens4, sig, axis=0), sig, axis=2).reshape(width, width)
        image = jnp.dot(p_ss, phi, preferred_element_type=jnp.float32)
        phif = phi.astype(jnp.float32)
        rho = jnp.maximum(jnp.sum(phif * image, axis=0), 0.0)
        root = jnp.cbrt(rho)
        energy = live * jnp.sum(weight * (-slater) * rho * root)
        scaled = (phif * (weight * (-4.0 / 3.0 * slater) * root)[None, :]).astype(jnp.bfloat16)
        delta = jnp.dot(phi, scaled.T, preferred_element_type=jnp.float32) * live
        delta = delta.reshape(NSIG, BLOCK, NSIG, BLOCK).transpose(0, 2, 1, 3)
        local = (sig - group * span).astype(jnp.int32)
        carry = carry.at[sig[:, None], :, local[None, :], :].add(delta)
        return carry, energy

    start = jnp.zeros((NBLK, BLOCK, span, BLOCK), jnp.float32)
    indices = jnp.arange(BATCHES, dtype=jnp.int32)
    out4, energies = lax.scan(step, start, (points, grid_weights, sig_blocks, indices))
    return out4.reshape(NBASIS, span * BLOCK), energies, jnp.sum(energies)
```

```python
import functools
import math

import jax
import jax.numpy as jnp
from jax import lax
from jax.experimental import pallas as pl
from jax.experimental.pallas import tpu as pltpu
from jax.sharding import PartitionSpec as P

BLOCK = 128
slater = 0.7386
LOG2E = 1.4426950408889634


def spread(value, axis, source):
    kept = jnp.where(lax.axis_index(axis) == source, value, 0).astype(value.dtype)
    return lax.psum(kept, axis)


def cut(value):
    return lax.reduce_precision(value, exponent_bits=8, mantissa_bits=7)


def function_terms(centres, exponents):
    a = exponents * LOG2E
    cc = jnp.sum(centres * centres, axis=0)
    zero = jnp.zeros_like(a)
    coef = jnp.stack(
        [2 * a * centres[0], 2 * a * centres[1], 2 * a * centres[2], -a, -a * cc, zero, zero, zero],
        axis=1,
    )
    hi = cut(coef)
    mid = cut(coef - hi)
    lo = cut(coef - hi - mid)
    return jnp.concatenate([hi, mid, lo, hi, mid, hi], axis=1).astype(jnp.bfloat16)


def point_terms(p):
    x, y, z = p[0:1], p[1:2], p[2:3]
    r2 = x * x + y * y + z * z
    one = jnp.ones_like(x)
    zero = jnp.zeros_like(x)
    v = jnp.concatenate([x, y, z, r2, one, zero, zero, zero], axis=0)
    hi = v.astype(jnp.bfloat16).astype(jnp.float32)
    rest = v - hi
    mid = rest.astype(jnp.bfloat16).astype(jnp.float32)
    lo = rest - mid
    return jnp.concatenate([hi, hi, hi, mid, mid, lo], axis=0).astype(jnp.bfloat16)


def phi_block(terms_ref, s, feats):
    rows = terms_ref[pl.ds(pl.multiple_of(s * BLOCK, BLOCK), BLOCK), :]
    arg = jnp.dot(rows, feats, preferred_element_type=jnp.float32)
    return jnp.exp2(arg).astype(jnp.bfloat16)


def potential_kernel(nsig, sig_ref, live_ref, diag_ref, pw_ref, terms_ref, wpot_ref, energy_ref, eps_ref):
    wpot_ref[...] = jnp.zeros_like(wpot_ref)
    eps_ref[...] = jnp.zeros_like(eps_ref)

    def step(k, carry):
        p = pw_ref[k]
        w = p[3:4]
        feats = point_terms(p)
        s = [sig_ref[k * nsig + i] for i in range(nsig)]
        phis = [phi_block(terms_ref, s[i], feats) for i in range(nsig)]
        phi = jnp.concatenate(phis, axis=0)
        rho = jnp.zeros_like(w)
        for i in range(nsig):
            rows = pl.ds(pl.multiple_of(s[i] * BLOCK, BLOCK), BLOCK)
            dens = jnp.concatenate(
                [diag_ref[rows, pl.ds(pl.multiple_of(s[j] * BLOCK, BLOCK), BLOCK)] for j in range(nsig)],
                axis=1,
            )
            image = jnp.dot(dens, phi, preferred_element_type=jnp.float32)
            rho += jnp.sum(phis[i].astype(jnp.float32) * image, axis=0, keepdims=True)
        rho = jnp.maximum(rho, 0.0)
        root = jnp.where(rho > 0.0, jnp.exp2(jnp.log2(jnp.where(rho > 0.0, rho, 1.0)) * (1.0 / 3.0)), 0.0)
        eps_ref[pl.ds(k, 1), :] = w * -slater * rho * root
        wpot_ref[pl.ds(k, 1), :] = (w * (-4.0 / 3.0 * slater)) * root
        return carry

    lax.fori_loop(0, live_ref[0], step, 0)
    energy_ref[...] = jnp.sum(eps_ref[...], axis=1, keepdims=True)


def strip_kernel(nsig, slots, piece, sig_ref, live_ref, col_ref, pw_ref, wpot_ref, terms_ref, out_ref, phi_ref, list_ref):
    strip = out_ref.shape[1]
    npiece = strip // piece
    start = col_ref[0]
    blocks, offs = [], []
    for q in range(npiece):
        at = start + q * piece
        blocks.append(at // BLOCK)
        offs.append(at - (at // BLOCK) * BLOCK)
    out_ref[...] = jnp.zeros_like(out_ref)

    def scan_device(d, n):
        def scan_slot(k, n):
            b = d * slots + k
            hit = jnp.bool_(False)
            for i in range(nsig):
                v = sig_ref[b * nsig + i]
                for q in range(npiece):
                    hit = hit | (v == blocks[q])
            list_ref[n] = b
            return n + hit.astype(jnp.int32)

        return lax.fori_loop(0, live_ref[d], scan_slot, n)

    total = lax.fori_loop(0, live_ref.shape[0], scan_device, jnp.int32(0))
    list_ref[total] = 0

    def one(index, half):
        b = list_ref[index]
        valid = index < total
        feats = point_terms(pw_ref[b])
        s = [sig_ref[b * nsig + i] for i in range(nsig)]
        phis = [phi_block(terms_ref, s[i], feats) for i in range(nsig)]
        for i in range(nsig):
            phi_ref[half, pl.ds(i * BLOCK, BLOCK), :] = phis[i]
        wpot = wpot_ref[pl.ds(b, 1), :]
        cols = []
        for q in range(npiece):
            pos = jnp.int32(0)
            have = jnp.bool_(False)
            for i in range(nsig):
                eq = s[i] == blocks[q]
                pos = jnp.where(eq, i, pos)
                have = have | eq
            on = (have & valid).astype(jnp.float32)
            rows = phi_ref[half, pl.ds(pl.multiple_of(pos * BLOCK + offs[q], piece), piece), :]
            cols.append((rows.astype(jnp.float32) * (wpot * on)).astype(jnp.bfloat16))
        scaled = jnp.concatenate(cols, axis=0)
        for i in range(nsig):
            delta = lax.dot_general(
                phis[i], scaled, (((1,), (1,)), ((), ())), preferred_element_type=jnp.float32
            )
            rows = pl.ds(pl.multiple_of(s[i] * BLOCK, BLOCK), BLOCK)
            out_ref[rows, :] += delta

    def step(t, carry):
        one(2 * t, 0)
        one(2 * t + 1, 1)
        return carry

    lax.fori_loop(0, (total + 1) // 2, step, 0)


def shards(density, points, grid_weights, centres, exponents, sig_blocks, live_count):
    nrows = lax.axis_size("rows")
    ncols = lax.axis_size("cols")
    group = lax.axis_index("rows")
    col = lax.axis_index("cols")
    nsig = sig_blocks.shape[1]
    slots, _, npts = points.shape
    own_width = density.shape[0]
    span = own_width // BLOCK
    strip = own_width // ncols
    piece = math.gcd(strip, BLOCK)
    ratio = ncols // nrows

    vmem = pl.BlockSpec(memory_space=pltpu.VMEM)
    smem = pl.BlockSpec(memory_space=pltpu.SMEM)
    params = pltpu.CompilerParams(vmem_limit_bytes=48 * 1024 * 1024)

    pieces = []
    for offset in range(ratio):
        pieces.append(spread(density, "cols", group * ratio + offset))
    diag = jnp.concatenate(pieces, axis=1)

    own_centres = lax.dynamic_slice_in_dim(centres, group * own_width, own_width, 1)
    own_expo = lax.dynamic_slice_in_dim(exponents, group * own_width, own_width, 0)
    terms = function_terms(own_centres, own_expo)
    pw = jnp.concatenate([points, grid_weights[:, None, :]], axis=1)
    local = (sig_blocks - group * span).reshape(-1)

    pw_all = lax.all_gather(pw, "cols", axis=0, tiled=True)
    sig_all = lax.all_gather(local, "cols", axis=0, tiled=True)
    live_all = lax.all_gather(live_count, "cols", axis=0, tiled=True)

    wpot, energy = pl.pallas_call(
        functools.partial(potential_kernel, nsig),
        out_shape=(
            jax.ShapeDtypeStruct((slots, npts), jnp.float32),
            jax.ShapeDtypeStruct((slots, 1), jnp.float32),
        ),
        in_specs=[smem, smem, vmem, vmem, vmem],
        out_specs=(vmem, vmem),
        scratch_shapes=[pltpu.VMEM((slots, npts), jnp.float32)],
        compiler_params=params,
        name="potential",
    )(local, live_count, diag, pw, terms)
    own_energy = energy.reshape(slots)

    wpot_all = lax.all_gather(wpot, "cols", axis=0, tiled=True)
    exc_total = lax.psum(jnp.sum(own_energy), ("rows", "cols"))

    xc_diag = pl.pallas_call(
        functools.partial(strip_kernel, nsig, slots, piece),
        out_shape=jax.ShapeDtypeStruct((own_width, strip), jnp.float32),
        in_specs=[smem, smem, smem, vmem, vmem, vmem],
        out_specs=vmem,
        scratch_shapes=[
            pltpu.VMEM((2, nsig * BLOCK, npts), jnp.bfloat16),
            pltpu.SMEM((ncols * slots + 2,), jnp.int32),
        ],
        compiler_params=params,
        name="strip",
    )(sig_all, live_all, (col * strip).reshape(1).astype(jnp.int32), pw_all, wpot_all, terms)
    return (xc_diag, own_energy, exc_total)


def solution(mesh):
    placed = (
        P("rows", "cols"),
        P(("rows", "cols"), None, None),
        P(("rows", "cols"), None),
        P(),
        P(),
        P(("rows", "cols"), None),
        P(("rows", "cols")),
    )
    return jax.shard_map(
        shards,
        mesh=mesh,
        in_specs=placed,
        out_specs=(P("rows", "cols"), P(("rows", "cols")), P()),
        check_vma=False,
    )
```

```python
import functools
import math

import jax
import jax.numpy as jnp
from jax import lax
from jax.experimental import pallas as pl
from jax.experimental.pallas import tpu as pltpu
from jax.sharding import PartitionSpec as P

BLOCK = 128
slater = 0.7386


def cut(value):
    return lax.reduce_precision(value, exponent_bits=8, mantissa_bits=7)


def function_terms(centres, exponents):
    a = exponents
    cc = jnp.sum(centres * centres, axis=0)
    zero = jnp.zeros_like(a)
    coef = jnp.stack(
        [2 * a * centres[0], 2 * a * centres[1], 2 * a * centres[2], -a, -a * cc, zero, zero, zero],
        axis=1,
    )
    hi = cut(coef)
    mid = cut(coef - hi)
    lo = cut(coef - hi - mid)
    return jnp.concatenate([hi, mid, lo, hi, mid, hi], axis=1).astype(jnp.bfloat16)


def point_terms(pts_ref, row):
    x, y, z = (pts_ref[axis, pl.ds(row, 1), :] for axis in range(3))
    r2 = x * x + y * y + z * z
    one = jnp.ones_like(x)
    zero = jnp.zeros_like(x)
    v = jnp.concatenate([x, y, z, r2, one, zero, zero, zero], axis=0)
    hi = v.astype(jnp.bfloat16).astype(jnp.float32)
    rest = v - hi
    mid = rest.astype(jnp.bfloat16).astype(jnp.float32)
    lo = rest - mid
    return jnp.concatenate([hi, hi, hi, mid, mid, lo], axis=0).astype(jnp.bfloat16)


def phi_block(terms_ref, s, feats):
    arg = jnp.dot(terms_ref[s], feats, preferred_element_type=jnp.float32)
    return jnp.exp(arg).astype(jnp.bfloat16)


def exchange_kernel(
    nrows, ncols, nsig, chunks, stride,
    sig_ref, dens_ref, pts_ref, w_ref, meta_ref, terms_ref,
    pts_all_ref, pot_all_ref, energy_ref, exc_ref,
    diag_ref, phi_ref, rho_ref, ebuf_ref,
    local_sem, ring_send, ring_recv, sib_send, sib_recv,
    pts_send, pts_recv, fan_send, fan_recv, pot_send, pot_recv, exc_send, exc_recv,
):
    group = lax.axis_index("rows")
    me = lax.axis_index("cols")
    slots, npts = w_ref.shape
    span = diag_ref.shape[0]
    held = dens_ref.shape[2] // BLOCK
    ratio = span // held
    nq = ncols // ratio
    lane, place = me % ratio, me // ratio

    def ring_of(q):
        return q // 2 * 2 + (q % 2 + q // 2) % 2 if nq % 2 == 0 else q

    direction = 1 - 2 * (lane % 2)
    ring = ring_of(place)
    after = ring_of((ring + direction + nq) % nq)
    dist = ((ring - ring_of(group)) * direction + 2 * nq) % nq

    barrier = pltpu.get_barrier_semaphore()
    for j in range(1, ncols):
        pl.semaphore_signal(
            barrier, inc=1, device_id=(group, (me + j) % ncols), device_id_type=pl.DeviceIdType.MESH
        )
    for j in range(1, nrows):
        pl.semaphore_signal(
            barrier, inc=1, device_id=((group + j) % nrows, me), device_id_type=pl.DeviceIdType.MESH
        )
    pl.semaphore_wait(barrier, ncols + nrows - 2)

    def remote(src, dst, send, recv, to_row, to_col):
        return pltpu.make_async_remote_copy(
            src_ref=src, dst_ref=dst, send_sem=send, recv_sem=recv,
            device_id=(to_row, to_col), device_id_type=pl.DeviceIdType.MESH,
        )

    @pl.when(dist == 0)
    def _():
        own = [
            pltpu.make_async_copy(
                dens_ref.at[:, :, pl.ds(j * BLOCK, BLOCK)], diag_ref.at[lane * held + j], local_sem.at[j]
            )
            for j in range(held)
        ]
        for copy in own:
            copy.start()
        for copy in own:
            copy.wait()

    cuts = chunks // span
    rows_per = BLOCK // cuts

    def part(c, which):
        return diag_ref.at[
            pl.ds(which * held, held), c // cuts, pl.ds(pl.multiple_of(c % cuts * rows_per, rows_per), rows_per)
        ]

    def ring_copy(c):
        return remote(part(c, lane), part(c, lane), ring_send.at[c], ring_recv.at[c], group, after * ratio + lane)

    def sib_copy(c, j, which):
        to = place * ratio + (lane + j) % ratio
        return remote(part(c, which), part(c, which), sib_send.at[j - 1, c], sib_recv.at[j - 1, c], group, to)

    per = slots // chunks
    mine = me * stride
    for axis in range(3):
        pts_all_ref[axis, pl.ds(pl.multiple_of(mine, 8), slots), :] = pts_ref[axis]

    def chunk_step(c, carry):
        @pl.when(dist > 0)
        def _():
            ring_copy(c).wait_recv()

        @pl.when(dist < nq - 1)
        def _():
            ring_copy(c).start()

        for j in range(1, ratio):
            sib_copy(c, j, lane).start()
        for u in range(per):
            k = c * per + u
            feats = point_terms(pts_ref, k)
            for i in range(nsig):
                at = pl.multiple_of((k * nsig + i) * BLOCK, BLOCK)
                phi_ref[pl.ds(at, BLOCK), :] = phi_block(terms_ref, sig_ref[k * nsig + i], feats)
        return carry

    lax.fori_loop(0, chunks, chunk_step, 0)

    def slab(which):
        return pts_all_ref.at[:, pl.ds(pl.multiple_of(which * stride, 8), slots), :]

    def pts_copy(j, owner):
        to = (me + j * ratio) % ncols
        return remote(slab(owner), slab(owner), pts_send.at[j - 1], pts_recv.at[j - 1], group, to)

    def fan_copy(j, l, owner):
        to = place * ratio + (lane + l) % ratio
        return remote(slab(owner), slab(owner), fan_send.at[l - 1, j], fan_recv.at[l - 1, j], group, to)

    for j in range(1, nq):
        pts_copy(j, me).start()
    for l in range(1, ratio):
        fan_copy(0, l, me).start()

    def drain(c, carry):
        for j in range(1, ratio):
            sib_copy(c, j, (lane + ratio - j) % ratio).wait_recv()
        return carry

    lax.fori_loop(0, chunks, drain, 0)

    def image_rho(k):
        s = [sig_ref[k * nsig + i] for i in range(nsig)]
        phi = phi_ref[pl.ds(pl.multiple_of(k * nsig * BLOCK, BLOCK), nsig * BLOCK), :]
        total = None
        for i in range(nsig):
            dens = jnp.concatenate([diag_ref[s[j], s[i]] for j in range(nsig)], axis=1)
            image = jnp.dot(dens, phi, preferred_element_type=jnp.float32)
            prod = phi[i * BLOCK : (i + 1) * BLOCK].astype(jnp.float32) * image
            prod = jnp.sum(prod.reshape(BLOCK // 8, 8, npts), axis=0)
            total = prod if total is None else total + prod
        return jnp.sum(total, axis=0, keepdims=True)

    def image_step(t, carry):
        first = image_rho(2 * t)
        second = image_rho(2 * t + 1)
        rho_ref[pl.ds(2 * t, 1), :] = first
        rho_ref[pl.ds(2 * t + 1, 1), :] = second
        return carry

    half = slots // 4
    lax.fori_loop(0, half, image_step, 0)

    for j in range(1, nq):
        owner = (me + ncols - j * ratio) % ncols
        pts_copy(j, owner).wait_recv()
        for l in range(1, ratio):
            fan_copy(j, l, owner).start()

    lax.fori_loop(half, slots // 2, image_step, 0)

    w = w_ref[...]
    rho = jnp.maximum(rho_ref[...], 0.0)
    above = rho > 0.0
    root = jnp.where(above, jnp.exp2(jnp.log2(jnp.where(above, rho, 1.0)) * (1.0 / 3.0)), 0.0)
    energy = jnp.sum(w * -slater * rho * root, axis=1, keepdims=True)
    energy_ref[...] = energy
    pot_all_ref[pl.ds(pl.multiple_of(mine, 8), slots), :] = (w * (-4.0 / 3.0 * slater)) * root
    own_sum = jnp.sum(energy, axis=0, keepdims=True)
    tail = lax.broadcasted_iota(jnp.int32, (8, npts), 0)
    pot_all_ref[pl.ds(pl.multiple_of(mine + slots, 8), 8), :] = jnp.where(
        tail == 0, jnp.broadcast_to(own_sum, (8, npts)), meta_ref[...]
    )

    def pot_slab(which):
        return pot_all_ref.at[pl.ds(pl.multiple_of(which * stride, 8), stride), :]

    def pot_copy(j, owner):
        return remote(pot_slab(owner), pot_slab(owner), pot_send.at[j - 1], pot_recv.at[j - 1], group, (me + j) % ncols)

    for j in range(1, ncols):
        pot_copy(j, me).start()

    def settle(c, carry):
        @pl.when(dist < nq - 1)
        def _():
            ring_copy(c).wait_send()

        for j in range(1, ratio):
            sib_copy(c, j, lane).wait_send()
        return carry

    lax.fori_loop(0, chunks, settle, 0)
    for j in range(1, nq):
        pts_copy(j, me).wait_send()
    for l in range(1, ratio):
        sibling = place * ratio + (lane + ratio - l) % ratio
        for j in range(nq):
            fan_copy(j, l, (me + ncols - j * ratio) % ncols).wait_send()
            fan_copy(j, l, (sibling + ncols - j * ratio) % ncols).wait_recv()
    for j in range(1, ncols):
        pot_copy(j, (me + ncols - j) % ncols).wait_recv()

    part_sum = jnp.zeros((8, BLOCK), jnp.float32)
    for d in range(ncols):
        part_sum += pot_all_ref[d * stride + slots : d * stride + slots + 1, 0:BLOCK]
    ebuf_ref[group] = part_sum

    def exc_copy(j, owner):
        return remote(ebuf_ref.at[owner], ebuf_ref.at[owner], exc_send.at[j - 1], exc_recv.at[j - 1], (group + j) % nrows, me)

    for j in range(1, nrows):
        exc_copy(j, group).start()
    for j in range(1, ncols):
        pot_copy(j, me).wait_send()
    for j in range(1, nrows):
        exc_copy(j, (group + nrows - j) % nrows).wait_recv()
    exc = jnp.zeros((8, BLOCK), jnp.float32)
    for g in range(nrows):
        exc += ebuf_ref[g]
    exc_ref[...] = exc
    for j in range(1, nrows):
        exc_copy(j, group).wait_send()


def strip_kernel(nsig, slots, stride, piece, sig_ref, live_ref, col_ref, pts_ref, wpot_ref, terms_ref, out_ref, phi_a, phi_b, list_ref):
    strip = out_ref.shape[1]
    npiece = strip // piece
    start = col_ref[0]
    blocks, offs = [], []
    for q in range(npiece):
        at = start + q * piece
        blocks.append(at // BLOCK)
        offs.append(at - (at // BLOCK) * BLOCK)
    out_ref[...] = jnp.zeros_like(out_ref)

    def scan_device(d, n):
        def scan_slot(k, n):
            b = d * slots + k
            hit = jnp.bool_(False)
            for i in range(nsig):
                v = sig_ref[b * nsig + i]
                for block in blocks:
                    hit = hit | (v == block)
            list_ref[n] = d * stride + k
            return n + hit.astype(jnp.int32)

        return lax.fori_loop(0, live_ref[d], scan_slot, n)

    total = lax.fori_loop(0, live_ref.shape[0], scan_device, jnp.int32(0))
    for extra in range(3):
        list_ref[total + extra] = 0

    def blocks_of(row):
        b = row - row // stride * (stride - slots)
        return [sig_ref[b * nsig + i] for i in range(nsig)]

    def make(index, dst):
        row = list_ref[index]
        feats = point_terms(pts_ref, row)
        s = blocks_of(row)
        for i in range(nsig):
            dst[pl.ds(i * BLOCK, BLOCK), :] = phi_block(terms_ref, s[i], feats)

    def add(index, src):
        row = list_ref[index]
        valid = index < total
        s = blocks_of(row)
        wpot = wpot_ref[pl.ds(row, 1), :]
        cols = []
        for q in range(npiece):
            pos = jnp.int32(0)
            have = jnp.bool_(False)
            for i in range(nsig):
                eq = s[i] == blocks[q]
                pos = jnp.where(eq, i, pos)
                have = have | eq
            on = (have & valid).astype(jnp.float32)
            rows = src[pl.ds(pl.multiple_of(pos * BLOCK + offs[q], piece), piece), :]
            cols.append((rows.astype(jnp.float32) * (wpot * on)).astype(jnp.bfloat16))
        scaled = jnp.concatenate(cols, axis=0)
        deltas = [
            lax.dot_general(
                src[pl.ds(i * BLOCK, BLOCK), :], scaled, (((1,), (1,)), ((), ())),
                preferred_element_type=jnp.float32,
            )
            for i in range(nsig)
        ]
        for i in range(nsig):
            rows = pl.ds(pl.multiple_of(s[i] * BLOCK, BLOCK), BLOCK)
            out_ref[rows, :] += deltas[i]

    make(0, phi_a)

    def step(t, carry):
        make(2 * t + 1, phi_b)
        add(2 * t, phi_a)
        make(2 * t + 2, phi_a)
        add(2 * t + 1, phi_b)
        return carry

    lax.fori_loop(0, (total + 1) // 2, step, 0)


def shards(density, points, grid_weights, centres, exponents, sig_blocks, live_count):
    nrows = lax.axis_size("rows")
    ncols = lax.axis_size("cols")
    group = lax.axis_index("rows")
    col = lax.axis_index("cols")
    nsig = sig_blocks.shape[1]
    slots, _, npts = points.shape
    own_width = density.shape[0]
    span = own_width // BLOCK
    strip = own_width // ncols
    piece = math.gcd(strip, BLOCK)
    ratio = own_width // density.shape[1]
    nq = ncols // ratio
    stride = slots + 8
    chunks = span * max(d for d in (1, 2, 4) if slots % (span * d) == 0)

    vmem = pl.BlockSpec(memory_space=pltpu.VMEM)
    smem = pl.BlockSpec(memory_space=pltpu.SMEM)
    hbm = pl.BlockSpec(memory_space=pl.ANY)

    own_centres = lax.dynamic_slice_in_dim(centres, group * own_width, own_width, 1)
    own_expo = lax.dynamic_slice_in_dim(exponents, group * own_width, own_width, 0)
    terms = function_terms(own_centres, own_expo).reshape(span, BLOCK, -1)
    live = jnp.arange(slots)[:, None] < live_count[0]
    weights = jnp.where(live, grid_weights, 0.0)
    local = (sig_blocks - group * span).reshape(-1)
    sig_row = jnp.pad(local, (0, npts - slots * nsig)).astype(jnp.float32)
    live_row = jnp.broadcast_to(live_count.astype(jnp.float32), (npts,))
    blank = jnp.zeros((npts,), jnp.float32)
    meta = jnp.stack([blank, sig_row, live_row] + [blank] * 5)

    dma = pltpu.SemaphoreType.DMA
    pts_all, pot_all, energy, exc = pl.pallas_call(
        functools.partial(exchange_kernel, nrows, ncols, nsig, chunks, stride),
        out_shape=(
            jax.ShapeDtypeStruct((3, ncols * stride, npts), jnp.float32),
            jax.ShapeDtypeStruct((ncols * stride, npts), jnp.float32),
            jax.ShapeDtypeStruct((slots, 1), jnp.float32),
            jax.ShapeDtypeStruct((8, BLOCK), jnp.float32),
        ),
        in_specs=[smem, hbm, vmem, vmem, vmem, vmem],
        out_specs=(vmem, vmem, vmem, vmem),
        scratch_shapes=[
            pltpu.VMEM((span, span, BLOCK, BLOCK), jnp.bfloat16),
            pltpu.VMEM((slots * nsig * BLOCK, npts), jnp.bfloat16),
            pltpu.VMEM((slots, npts), jnp.float32),
            pltpu.VMEM((nrows, 8, BLOCK), jnp.float32),
            dma((span // ratio,)),
            dma((chunks,)),
            dma((chunks,)),
            dma((max(ratio - 1, 1), chunks)),
            dma((max(ratio - 1, 1), chunks)),
            dma((max(nq - 1, 1),)),
            dma((max(nq - 1, 1),)),
            dma((max(ratio - 1, 1), nq)),
            dma((max(ratio - 1, 1), nq)),
            dma((max(ncols - 1, 1),)),
            dma((max(ncols - 1, 1),)),
            dma((max(nrows - 1, 1),)),
            dma((max(nrows - 1, 1),)),
        ],
        compiler_params=pltpu.CompilerParams(
            collective_id=0, has_side_effects=True, vmem_limit_bytes=48 * 1024 * 1024
        ),
        name="exchange",
    )(local, density.reshape(span, BLOCK, -1), points.transpose(1, 0, 2), weights, meta, terms)
    own_energy = energy.reshape(slots)
    tails = pot_all.reshape(ncols, stride, npts)[:, slots : slots + 8]
    sig_all = tails[:, 1, : slots * nsig].astype(jnp.int32).reshape(-1)
    live_all = tails[:, 2, 0].astype(jnp.int32)

    xc_diag = pl.pallas_call(
        functools.partial(strip_kernel, nsig, slots, stride, piece),
        out_shape=jax.ShapeDtypeStruct((own_width, strip), jnp.float32),
        in_specs=[smem, smem, smem, vmem, vmem, vmem],
        out_specs=vmem,
        scratch_shapes=[
            pltpu.VMEM((nsig * BLOCK, npts), jnp.bfloat16),
            pltpu.VMEM((nsig * BLOCK, npts), jnp.bfloat16),
            pltpu.SMEM((ncols * slots + 8,), jnp.int32),
        ],
        compiler_params=pltpu.CompilerParams(vmem_limit_bytes=32 * 1024 * 1024),
        name="strip",
    )(sig_all, live_all, (col * strip).reshape(1).astype(jnp.int32), pts_all, pot_all, terms)
    return (xc_diag, own_energy, exc[0, 0])


def solution(mesh):
    placed = (
        P("rows", "cols"),
        P(("rows", "cols"), None, None),
        P(("rows", "cols"), None),
        P(),
        P(),
        P(("rows", "cols"), None),
        P(("rows", "cols")),
    )
    return jax.shard_map(
        shards,
        mesh=mesh,
        in_specs=placed,
        out_specs=(P("rows", "cols"), P(("rows", "cols")), P()),
        check_vma=False,
    )
```

```python
import functools
import math

import jax
import jax.numpy as jnp
from jax import lax
from jax.experimental import pallas as pl
from jax.experimental.pallas import tpu as pltpu
from jax.sharding import PartitionSpec as P

BLOCK = 128
slater = 0.7386


def cut(value):
    return lax.reduce_precision(value, exponent_bits=8, mantissa_bits=7)


def function_terms(centres, exponents):
    a = exponents
    cc = jnp.sum(centres * centres, axis=0)
    zero = jnp.zeros_like(a)
    coef = jnp.stack(
        [2 * a * centres[0], 2 * a * centres[1], 2 * a * centres[2], -a, -a * cc, zero, zero, zero],
        axis=1,
    )
    hi = cut(coef)
    mid = cut(coef - hi)
    lo = cut(coef - hi - mid)
    return jnp.concatenate([hi, mid, lo, hi, mid, hi], axis=1).astype(jnp.bfloat16)


def point_terms(pts_ref, row):
    x, y, z = (pts_ref[axis, pl.ds(row, 1), :] for axis in range(3))
    r2 = x * x + y * y + z * z
    one = jnp.ones_like(x)
    zero = jnp.zeros_like(x)
    v = jnp.concatenate([x, y, z, r2, one, zero, zero, zero], axis=0)
    hi = v.astype(jnp.bfloat16).astype(jnp.float32)
    rest = v - hi
    mid = rest.astype(jnp.bfloat16).astype(jnp.float32)
    lo = rest - mid
    return jnp.concatenate([hi, hi, hi, mid, mid, lo], axis=0).astype(jnp.bfloat16)


def phi_rows(terms_ref, s, feats):
    terms = jnp.concatenate([terms_ref[v] for v in s], axis=0)
    arg = jnp.dot(terms, feats, preferred_element_type=jnp.float32)
    return jnp.exp(arg).astype(jnp.bfloat16)


def exchange_kernel(
    nrows, ncols, nsig, chunks, stride,
    sig_ref, dens_ref, pts_ref, w_ref, meta_ref, terms_ref,
    pts_all_ref, pot_all_ref, energy_ref, exc_ref,
    diag_ref, phi_ref, rho_ref, ebuf_ref,
    local_sem, ring_send, ring_recv, sib_send, sib_recv,
    pts_send, pts_recv, fan_send, fan_recv, pot_send, pot_recv, exc_send, exc_recv,
):
    group = lax.axis_index("rows")
    me = lax.axis_index("cols")
    slots, npts = w_ref.shape
    span = diag_ref.shape[0]
    held = dens_ref.shape[2] // BLOCK
    ratio = span // held
    nq = ncols // ratio
    lane, place = me % ratio, me // ratio

    def ring_of(q):
        return q // 2 * 2 + (q % 2 + q // 2) % 2 if nq % 2 == 0 else q

    direction = 1 - 2 * (lane % 2)
    ring = ring_of(place)
    after = ring_of((ring + direction + nq) % nq)
    dist = ((ring - ring_of(group)) * direction + 2 * nq) % nq

    barrier = pltpu.get_barrier_semaphore()
    for j in range(1, ncols):
        pl.semaphore_signal(
            barrier, inc=1, device_id=(group, (me + j) % ncols), device_id_type=pl.DeviceIdType.MESH
        )
    for j in range(1, nrows):
        pl.semaphore_signal(
            barrier, inc=1, device_id=((group + j) % nrows, me), device_id_type=pl.DeviceIdType.MESH
        )
    pl.semaphore_wait(barrier, ncols + nrows - 2)

    def remote(src, dst, send, recv, to_row, to_col):
        return pltpu.make_async_remote_copy(
            src_ref=src, dst_ref=dst, send_sem=send, recv_sem=recv,
            device_id=(to_row, to_col), device_id_type=pl.DeviceIdType.MESH,
        )

    @pl.when(dist == 0)
    def _():
        own = [
            pltpu.make_async_copy(
                dens_ref.at[:, :, pl.ds(j * BLOCK, BLOCK)], diag_ref.at[lane * held + j], local_sem.at[j]
            )
            for j in range(held)
        ]
        for copy in own:
            copy.start()
        for copy in own:
            copy.wait()

    cuts = chunks // span
    rows_per = BLOCK // cuts

    def part(c, which):
        return diag_ref.at[
            pl.ds(which * held, held), c // cuts, pl.ds(pl.multiple_of(c % cuts * rows_per, rows_per), rows_per)
        ]

    def ring_copy(c):
        return remote(part(c, lane), part(c, lane), ring_send.at[c], ring_recv.at[c], group, after * ratio + lane)

    def sib_copy(c, j, which):
        to = place * ratio + (lane + j) % ratio
        return remote(part(c, which), part(c, which), sib_send.at[j - 1, c], sib_recv.at[j - 1, c], group, to)

    per = slots // chunks
    mine = me * stride
    for axis in range(3):
        pts_all_ref[axis, pl.ds(pl.multiple_of(mine, 8), slots), :] = pts_ref[axis]

    def chunk_step(c, carry):
        @pl.when(dist > 0)
        def _():
            ring_copy(c).wait_recv()

        @pl.when(dist < nq - 1)
        def _():
            ring_copy(c).start()

        for j in range(1, ratio):
            sib_copy(c, j, lane).start()
        for u in range(per):
            k = c * per + u
            feats = point_terms(pts_ref, k)
            s = [sig_ref[k * nsig + i] for i in range(nsig)]
            at = pl.multiple_of(k * nsig * BLOCK, nsig * BLOCK)
            phi_ref[pl.ds(at, nsig * BLOCK), :] = phi_rows(terms_ref, s, feats)
        return carry

    lax.fori_loop(0, chunks, chunk_step, 0)

    def slab(which):
        return pts_all_ref.at[:, pl.ds(pl.multiple_of(which * stride, 8), slots), :]

    def pts_copy(j, owner):
        to = (me + j * ratio) % ncols
        return remote(slab(owner), slab(owner), pts_send.at[j - 1], pts_recv.at[j - 1], group, to)

    def fan_copy(j, l, owner):
        to = place * ratio + (lane + l) % ratio
        return remote(slab(owner), slab(owner), fan_send.at[l - 1, j], fan_recv.at[l - 1, j], group, to)

    for j in range(1, nq):
        pts_copy(j, me).start()
    for l in range(1, ratio):
        fan_copy(0, l, me).start()

    def drain(c, carry):
        for j in range(1, ratio):
            sib_copy(c, j, (lane + ratio - j) % ratio).wait_recv()
        return carry

    lax.fori_loop(0, chunks, drain, 0)

    def image_rho(k):
        s = [sig_ref[k * nsig + i] for i in range(nsig)]
        phi = phi_ref[pl.ds(pl.multiple_of(k * nsig * BLOCK, BLOCK), nsig * BLOCK), :]
        dens = jnp.concatenate(
            [jnp.concatenate([diag_ref[s[j], s[i]] for j in range(nsig)], axis=1) for i in range(nsig)], axis=0
        )
        image = jnp.dot(dens, phi, preferred_element_type=jnp.float32)
        prod = phi.astype(jnp.float32) * image
        total = jnp.sum(prod.reshape(nsig * BLOCK // 8, 8, npts), axis=0)
        return jnp.sum(total, axis=0, keepdims=True)

    def image_step(t, carry):
        first = image_rho(2 * t)
        second = image_rho(2 * t + 1)
        rho_ref[pl.ds(2 * t, 1), :] = first
        rho_ref[pl.ds(2 * t + 1, 1), :] = second
        return carry

    half = slots // 4
    lax.fori_loop(0, half, image_step, 0)

    for j in range(1, nq):
        owner = (me + ncols - j * ratio) % ncols
        pts_copy(j, owner).wait_recv()
        for l in range(1, ratio):
            fan_copy(j, l, owner).start()

    lax.fori_loop(half, slots // 2, image_step, 0)

    w = w_ref[...]
    rho = jnp.maximum(rho_ref[...], 0.0)
    above = rho > 0.0
    root = jnp.where(above, jnp.exp2(jnp.log2(jnp.where(above, rho, 1.0)) * (1.0 / 3.0)), 0.0)
    energy = jnp.sum(w * -slater * rho * root, axis=1, keepdims=True)
    energy_ref[...] = energy
    pot_all_ref[pl.ds(pl.multiple_of(mine, 8), slots), :] = (w * (-4.0 / 3.0 * slater)) * root
    own_sum = jnp.sum(energy, axis=0, keepdims=True)
    tail = lax.broadcasted_iota(jnp.int32, (8, npts), 0)
    pot_all_ref[pl.ds(pl.multiple_of(mine + slots, 8), 8), :] = jnp.where(
        tail == 0, jnp.broadcast_to(own_sum, (8, npts)), meta_ref[...]
    )

    def pot_slab(which):
        return pot_all_ref.at[pl.ds(pl.multiple_of(which * stride, 8), stride), :]

    def pot_copy(j, owner):
        return remote(pot_slab(owner), pot_slab(owner), pot_send.at[j - 1], pot_recv.at[j - 1], group, (me + j) % ncols)

    for j in range(1, ncols):
        pot_copy(j, me).start()

    def settle(c, carry):
        @pl.when(dist < nq - 1)
        def _():
            ring_copy(c).wait_send()

        for j in range(1, ratio):
            sib_copy(c, j, lane).wait_send()
        return carry

    lax.fori_loop(0, chunks, settle, 0)
    for j in range(1, nq):
        pts_copy(j, me).wait_send()
    for l in range(1, ratio):
        sibling = place * ratio + (lane + ratio - l) % ratio
        for j in range(nq):
            fan_copy(j, l, (me + ncols - j * ratio) % ncols).wait_send()
            fan_copy(j, l, (sibling + ncols - j * ratio) % ncols).wait_recv()
    for j in range(1, ncols):
        pot_copy(j, (me + ncols - j) % ncols).wait_recv()

    part_sum = jnp.zeros((8, BLOCK), jnp.float32)
    for d in range(ncols):
        part_sum += pot_all_ref[d * stride + slots : d * stride + slots + 1, 0:BLOCK]
    ebuf_ref[group] = part_sum

    def exc_copy(j, owner):
        return remote(ebuf_ref.at[owner], ebuf_ref.at[owner], exc_send.at[j - 1], exc_recv.at[j - 1], (group + j) % nrows, me)

    for j in range(1, nrows):
        exc_copy(j, group).start()
    for j in range(1, ncols):
        pot_copy(j, me).wait_send()
    for j in range(1, nrows):
        exc_copy(j, (group + nrows - j) % nrows).wait_recv()
    exc = jnp.zeros((8, BLOCK), jnp.float32)
    for g in range(nrows):
        exc += ebuf_ref[g]
    exc_ref[...] = exc
    for j in range(1, nrows):
        exc_copy(j, group).wait_send()


def strip_kernel(nsig, slots, stride, piece, sig_ref, live_ref, col_ref, pts_ref, wpot_ref, terms_ref, out_ref, phi_a, phi_b, list_ref):
    strip = out_ref.shape[1]
    npiece = strip // piece
    start = col_ref[0]
    blocks, offs = [], []
    for q in range(npiece):
        at = start + q * piece
        blocks.append(at // BLOCK)
        offs.append(at - (at // BLOCK) * BLOCK)
    out_ref[...] = jnp.zeros_like(out_ref)

    def scan_device(d, n):
        def scan_slot(k, n):
            b = d * slots + k
            hit = jnp.bool_(False)
            for i in range(nsig):
                v = sig_ref[b * nsig + i]
                for block in blocks:
                    hit = hit | (v == block)
            list_ref[n] = d * stride + k
            return n + hit.astype(jnp.int32)

        return lax.fori_loop(0, live_ref[d], scan_slot, n)

    total = lax.fori_loop(0, live_ref.shape[0], scan_device, jnp.int32(0))
    for extra in range(3):
        list_ref[total + extra] = 0

    def blocks_of(row):
        b = row - row // stride * (stride - slots)
        return [sig_ref[b * nsig + i] for i in range(nsig)]

    def make(index, dst):
        row = list_ref[index]
        feats = point_terms(pts_ref, row)
        s = blocks_of(row)
        dst[...] = phi_rows(terms_ref, s, feats)

    def add(index, src):
        row = list_ref[index]
        valid = index < total
        s = blocks_of(row)
        wpot = wpot_ref[pl.ds(row, 1), :]
        cols = []
        for q in range(npiece):
            pos = jnp.int32(0)
            have = jnp.bool_(False)
            for i in range(nsig):
                eq = s[i] == blocks[q]
                pos = jnp.where(eq, i, pos)
                have = have | eq
            on = (have & valid).astype(jnp.float32)
            rows = src[pl.ds(pl.multiple_of(pos * BLOCK + offs[q], piece), piece), :]
            cols.append((rows.astype(jnp.float32) * (wpot * on)).astype(jnp.bfloat16))
        scaled = jnp.concatenate(cols, axis=0)
        delta = lax.dot_general(
            src[...], scaled, (((1,), (1,)), ((), ())), preferred_element_type=jnp.float32
        )
        for i in range(nsig):
            rows = pl.ds(pl.multiple_of(s[i] * BLOCK, BLOCK), BLOCK)
            out_ref[rows, :] += delta[i * BLOCK : (i + 1) * BLOCK]

    make(0, phi_a)

    def step(t, carry):
        make(2 * t + 1, phi_b)
        add(2 * t, phi_a)
        make(2 * t + 2, phi_a)
        add(2 * t + 1, phi_b)
        return carry

    lax.fori_loop(0, (total + 1) // 2, step, 0)


def shards(density, points, grid_weights, centres, exponents, sig_blocks, live_count):
    nrows = lax.axis_size("rows")
    ncols = lax.axis_size("cols")
    group = lax.axis_index("rows")
    col = lax.axis_index("cols")
    nsig = sig_blocks.shape[1]
    slots, _, npts = points.shape
    own_width = density.shape[0]
    span = own_width // BLOCK
    strip = own_width // ncols
    piece = math.gcd(strip, BLOCK)
    ratio = own_width // density.shape[1]
    nq = ncols // ratio
    stride = slots + 8
    chunks = span * max(d for d in (1, 2, 4) if slots % (span * d) == 0)

    vmem = pl.BlockSpec(memory_space=pltpu.VMEM)
    smem = pl.BlockSpec(memory_space=pltpu.SMEM)
    hbm = pl.BlockSpec(memory_space=pl.ANY)

    own_centres = lax.dynamic_slice_in_dim(centres, group * own_width, own_width, 1)
    own_expo = lax.dynamic_slice_in_dim(exponents, group * own_width, own_width, 0)
    terms = function_terms(own_centres, own_expo).reshape(span, BLOCK, -1)
    live = jnp.arange(slots)[:, None] < live_count[0]
    weights = jnp.where(live, grid_weights, 0.0)
    local = (sig_blocks - group * span).reshape(-1)
    sig_row = jnp.pad(local, (0, npts - slots * nsig)).astype(jnp.float32)
    live_row = jnp.broadcast_to(live_count.astype(jnp.float32), (npts,))
    blank = jnp.zeros((npts,), jnp.float32)
    meta = jnp.stack([blank, sig_row, live_row] + [blank] * 5)

    dma = pltpu.SemaphoreType.DMA
    pts_all, pot_all, energy, exc = pl.pallas_call(
        functools.partial(exchange_kernel, nrows, ncols, nsig, chunks, stride),
        out_shape=(
            jax.ShapeDtypeStruct((3, ncols * stride, npts), jnp.float32),
            jax.ShapeDtypeStruct((ncols * stride, npts), jnp.float32),
            jax.ShapeDtypeStruct((slots, 1), jnp.float32),
            jax.ShapeDtypeStruct((8, BLOCK), jnp.float32),
        ),
        in_specs=[smem, hbm, vmem, vmem, vmem, vmem],
        out_specs=(vmem, vmem, vmem, vmem),
        scratch_shapes=[
            pltpu.VMEM((span, span, BLOCK, BLOCK), jnp.bfloat16),
            pltpu.VMEM((slots * nsig * BLOCK, npts), jnp.bfloat16),
            pltpu.VMEM((slots, npts), jnp.float32),
            pltpu.VMEM((nrows, 8, BLOCK), jnp.float32),
            dma((span // ratio,)),
            dma((chunks,)),
            dma((chunks,)),
            dma((max(ratio - 1, 1), chunks)),
            dma((max(ratio - 1, 1), chunks)),
            dma((max(nq - 1, 1),)),
            dma((max(nq - 1, 1),)),
            dma((max(ratio - 1, 1), nq)),
            dma((max(ratio - 1, 1), nq)),
            dma((max(ncols - 1, 1),)),
            dma((max(ncols - 1, 1),)),
            dma((max(nrows - 1, 1),)),
            dma((max(nrows - 1, 1),)),
        ],
        compiler_params=pltpu.CompilerParams(
            collective_id=0, has_side_effects=True, vmem_limit_bytes=48 * 1024 * 1024
        ),
        name="exchange",
    )(local, density.reshape(span, BLOCK, -1), points.transpose(1, 0, 2), weights, meta, terms)
    own_energy = energy.reshape(slots)
    tails = pot_all.reshape(ncols, stride, npts)[:, slots : slots + 8]
    sig_all = tails[:, 1, : slots * nsig].astype(jnp.int32).reshape(-1)
    live_all = tails[:, 2, 0].astype(jnp.int32)

    xc_diag = pl.pallas_call(
        functools.partial(strip_kernel, nsig, slots, stride, piece),
        out_shape=jax.ShapeDtypeStruct((own_width, strip), jnp.float32),
        in_specs=[smem, smem, smem, vmem, vmem, vmem],
        out_specs=vmem,
        scratch_shapes=[
            pltpu.VMEM((nsig * BLOCK, npts), jnp.bfloat16),
            pltpu.VMEM((nsig * BLOCK, npts), jnp.bfloat16),
            pltpu.SMEM((ncols * slots + 8,), jnp.int32),
        ],
        compiler_params=pltpu.CompilerParams(vmem_limit_bytes=32 * 1024 * 1024),
        name="strip",
    )(sig_all, live_all, (col * strip).reshape(1).astype(jnp.int32), pts_all, pot_all, terms)
    return (xc_diag, own_energy, exc[0, 0])


def solution(mesh):
    placed = (
        P("rows", "cols"),
        P(("rows", "cols"), None, None),
        P(("rows", "cols"), None),
        P(),
        P(),
        P(("rows", "cols"), None),
        P(("rows", "cols")),
    )
    return jax.shard_map(
        shards,
        mesh=mesh,
        in_specs=placed,
        out_specs=(P("rows", "cols"), P(("rows", "cols")), P()),
        check_vma=False,
    )
```

```python
import functools
import math

import jax
import jax.numpy as jnp
from jax import lax
from jax.experimental import pallas as pl
from jax.experimental.pallas import tpu as pltpu
from jax.sharding import PartitionSpec as P

BLOCK = 128
slater = 0.7386


def function_terms(c, a):
    cc = c[0:1] * c[0:1] + c[1:2] * c[1:2] + c[2:3] * c[2:3]
    coef = jnp.concatenate([2.0 * a * c, -a, -a * cc, jnp.zeros_like(c)], axis=0)
    hi = coef.astype(jnp.bfloat16).astype(jnp.float32)
    rest = coef - hi
    mid = rest.astype(jnp.bfloat16).astype(jnp.float32)
    lo = rest - mid
    return jnp.concatenate([hi, mid, lo, hi, mid, hi], axis=0).T.astype(jnp.bfloat16)


def point_terms(pts_ref, row):
    x, y, z = (pts_ref[axis, pl.ds(row, 1), :] for axis in range(3))
    r2 = x * x + y * y + z * z
    one = jnp.ones_like(x)
    zero = jnp.zeros_like(x)
    v = jnp.concatenate([x, y, z, r2, one, zero, zero, zero], axis=0)
    hi = v.astype(jnp.bfloat16).astype(jnp.float32)
    rest = v - hi
    mid = rest.astype(jnp.bfloat16).astype(jnp.float32)
    lo = rest - mid
    return jnp.concatenate([hi, hi, hi, mid, mid, lo], axis=0).astype(jnp.bfloat16)


def phi_rows(terms_ref, s, feats):
    terms = jnp.concatenate([terms_ref[v] for v in s], axis=0)
    arg = jnp.dot(terms, feats, preferred_element_type=jnp.float32)
    return jnp.exp(arg).astype(jnp.bfloat16)


def exchange_kernel(
    nrows, ncols, nsig, chunks, stride,
    sig_ref, live_ref, sig_rows_ref, dens_ref, pts_ref, w_ref, centres_ref, expo_ref,
    pts_all_ref, pot_all_ref, energy_ref, exc_ref, terms_ref,
    diag_ref, phi_ref, rho_ref, ebuf_ref, meta_ref,
    local_sem, ring_send, ring_recv, sib_send, sib_recv,
    pts_send, pts_recv, fan_send, fan_recv, pot_send, pot_recv, exc_send, exc_recv,
):
    group = lax.axis_index("rows")
    me = lax.axis_index("cols")
    slots, npts = w_ref.shape
    span = diag_ref.shape[0]
    held = dens_ref.shape[2] // BLOCK
    ratio = span // held
    nq = ncols // ratio
    lane, place = me % ratio, me // ratio

    def ring_of(q):
        return q // 2 * 2 + (q % 2 + q // 2) % 2 if nq % 2 == 0 else q

    direction = 1 - 2 * (lane % 2)
    ring = ring_of(place)
    after = ring_of((ring + direction + nq) % nq)
    dist = ((ring - ring_of(group)) * direction + 2 * nq) % nq

    barrier = pltpu.get_barrier_semaphore()
    for j in range(1, ncols):
        pl.semaphore_signal(
            barrier, inc=1, device_id=(group, (me + j) % ncols), device_id_type=pl.DeviceIdType.MESH
        )
    for j in range(1, nrows):
        pl.semaphore_signal(
            barrier, inc=1, device_id=((group + j) % nrows, me), device_id_type=pl.DeviceIdType.MESH
        )

    base = group * span
    for j in range(span):
        at = pl.ds(pl.multiple_of((base + j) * BLOCK, BLOCK), BLOCK)
        terms_ref[j] = function_terms(centres_ref[:, at], expo_ref[:, at])
    live = live_ref[0].astype(jnp.float32)
    meta_ref[...] = jnp.zeros_like(meta_ref)
    meta_ref[1 : 1 + nsig, 0:slots] = sig_rows_ref[...].astype(jnp.float32)
    meta_ref[1 + nsig : 2 + nsig, :] = jnp.full((1, npts), live, jnp.float32)

    pl.semaphore_wait(barrier, ncols + nrows - 2)

    def remote(src, dst, send, recv, to_row, to_col):
        return pltpu.make_async_remote_copy(
            src_ref=src, dst_ref=dst, send_sem=send, recv_sem=recv,
            device_id=(to_row, to_col), device_id_type=pl.DeviceIdType.MESH,
        )

    @pl.when(dist == 0)
    def _():
        own = [
            pltpu.make_async_copy(
                dens_ref.at[:, :, pl.ds(j * BLOCK, BLOCK)], diag_ref.at[:, lane * held + j], local_sem.at[j]
            )
            for j in range(held)
        ]
        for copy in own:
            copy.start()
        for copy in own:
            copy.wait()

    cuts = chunks // span
    some = held // cuts

    def part(c, which):
        return diag_ref.at[c // cuts, pl.ds(which * held + c % cuts * some, some)]

    def ring_copy(c):
        return remote(part(c, lane), part(c, lane), ring_send.at[c], ring_recv.at[c], group, after * ratio + lane)

    def sib_copy(c, j, which):
        to = place * ratio + (lane + j) % ratio
        return remote(part(c, which), part(c, which), sib_send.at[j - 1, c], sib_recv.at[j - 1, c], group, to)

    per = slots // chunks
    mine = me * stride
    for axis in range(3):
        pts_all_ref[axis, pl.ds(pl.multiple_of(mine, 8), slots), :] = pts_ref[axis]

    def chunk_step(c, carry):
        @pl.when(dist > 0)
        def _():
            ring_copy(c).wait_recv()

        @pl.when(dist < nq - 1)
        def _():
            ring_copy(c).start()

        for j in range(1, ratio):
            sib_copy(c, j, lane).start()
        for u in range(per):
            k = c * per + u
            feats = point_terms(pts_ref, k)
            s = [jnp.maximum(sig_ref[i, k] - base, 0) for i in range(nsig)]
            at = pl.multiple_of(k * nsig * BLOCK, nsig * BLOCK)
            phi_ref[pl.ds(at, nsig * BLOCK), :] = phi_rows(terms_ref, s, feats)
        return carry

    lax.fori_loop(0, chunks, chunk_step, 0)

    def slab(which):
        return pts_all_ref.at[:, pl.ds(pl.multiple_of(which * stride, 8), slots), :]

    def pts_copy(j, owner):
        to = (me + j * ratio) % ncols
        return remote(slab(owner), slab(owner), pts_send.at[j - 1], pts_recv.at[j - 1], group, to)

    def fan_copy(j, l, owner):
        to = place * ratio + (lane + l) % ratio
        return remote(slab(owner), slab(owner), fan_send.at[l - 1, j], fan_recv.at[l - 1, j], group, to)

    for j in range(1, nq):
        pts_copy(j, me).start()
    for l in range(1, ratio):
        fan_copy(0, l, me).start()

    def drain(c, carry):
        for j in range(1, ratio):
            sib_copy(c, j, (lane + ratio - j) % ratio).wait_recv()
        return carry

    lax.fori_loop(0, chunks, drain, 0)

    def image_rho(k):
        s = [jnp.maximum(sig_ref[i, k] - base, 0) for i in range(nsig)]
        phi = phi_ref[pl.ds(pl.multiple_of(k * nsig * BLOCK, BLOCK), nsig * BLOCK), :]
        dens = jnp.concatenate(
            [jnp.concatenate([diag_ref[s[i], s[j]] for j in range(nsig)], axis=1) for i in range(nsig)], axis=0
        )
        image = jnp.dot(dens, phi, preferred_element_type=jnp.float32)
        prod = phi.astype(jnp.float32) * image
        total = jnp.sum(prod.reshape(nsig * BLOCK // 8, 8, npts), axis=0)
        return jnp.sum(total, axis=0, keepdims=True)

    def image_step(t, carry):
        first = image_rho(2 * t)
        second = image_rho(2 * t + 1)
        rho_ref[pl.ds(2 * t, 1), :] = first
        rho_ref[pl.ds(2 * t + 1, 1), :] = second
        return carry

    half = slots // 4
    lax.fori_loop(0, half, image_step, 0)

    for j in range(1, nq):
        owner = (me + ncols - j * ratio) % ncols
        pts_copy(j, owner).wait_recv()
        for l in range(1, ratio):
            fan_copy(j, l, owner).start()

    lax.fori_loop(half, slots // 2, image_step, 0)

    slot = lax.broadcasted_iota(jnp.int32, (slots, npts), 0).astype(jnp.float32)
    w = w_ref[...] * jnp.clip(live - slot, 0.0, 1.0)
    rho = jnp.maximum(rho_ref[...], 0.0)
    above = rho > 0.0
    root = jnp.where(above, jnp.exp2(jnp.log2(jnp.where(above, rho, 1.0)) * (1.0 / 3.0)), 0.0)
    energy = jnp.sum(w * -slater * rho * root, axis=1, keepdims=True)
    energy_ref[...] = energy
    pot_all_ref[pl.ds(pl.multiple_of(mine, 8), slots), :] = (w * (-4.0 / 3.0 * slater)) * root
    own_sum = jnp.sum(energy, axis=0, keepdims=True)
    tail = lax.broadcasted_iota(jnp.int32, (8, npts), 0)
    pot_all_ref[pl.ds(pl.multiple_of(mine + slots, 8), 8), :] = jnp.where(
        tail == 0, jnp.broadcast_to(own_sum, (8, npts)), meta_ref[...]
    )

    def pot_slab(which):
        return pot_all_ref.at[pl.ds(pl.multiple_of(which * stride, 8), stride), :]

    def pot_copy(j, owner):
        return remote(pot_slab(owner), pot_slab(owner), pot_send.at[j - 1], pot_recv.at[j - 1], group, (me + j) % ncols)

    for j in range(1, ncols):
        pot_copy(j, me).start()

    def settle(c, carry):
        @pl.when(dist < nq - 1)
        def _():
            ring_copy(c).wait_send()

        for j in range(1, ratio):
            sib_copy(c, j, lane).wait_send()
        return carry

    lax.fori_loop(0, chunks, settle, 0)
    for j in range(1, nq):
        pts_copy(j, me).wait_send()
    for l in range(1, ratio):
        sibling = place * ratio + (lane + ratio - l) % ratio
        for j in range(nq):
            fan_copy(j, l, (me + ncols - j * ratio) % ncols).wait_send()
            fan_copy(j, l, (sibling + ncols - j * ratio) % ncols).wait_recv()
    for j in range(1, ncols):
        pot_copy(j, (me + ncols - j) % ncols).wait_recv()

    part_sum = jnp.zeros((8, BLOCK), jnp.float32)
    for d in range(ncols):
        part_sum += pot_all_ref[d * stride + slots : d * stride + slots + 1, 0:BLOCK]
    ebuf_ref[group] = part_sum

    def exc_copy(j, owner):
        return remote(ebuf_ref.at[owner], ebuf_ref.at[owner], exc_send.at[j - 1], exc_recv.at[j - 1], (group + j) % nrows, me)

    for j in range(1, nrows):
        exc_copy(j, group).start()
    for j in range(1, ncols):
        pot_copy(j, me).wait_send()
    for j in range(1, nrows):
        exc_copy(j, (group + nrows - j) % nrows).wait_recv()
    exc = jnp.zeros((8, BLOCK), jnp.float32)
    for g in range(nrows):
        exc += ebuf_ref[g]
    exc_ref[...] = exc
    for j in range(1, nrows):
        exc_copy(j, group).wait_send()


def strip_kernel(nsig, slots, stride, piece, sig_ref, live_ref, col_ref, pts_ref, wpot_ref, terms_ref, out_ref, phi_a, phi_b, list_ref):
    strip = out_ref.shape[1]
    npiece = strip // piece
    start = col_ref[0]
    blocks, offs = [], []
    for q in range(npiece):
        at = start + q * piece
        blocks.append(at // BLOCK)
        offs.append(at - (at // BLOCK) * BLOCK)
    out_ref[...] = jnp.zeros_like(out_ref)

    def scan_device(d, n):
        def scan_slot(k, n):
            hit = jnp.bool_(False)
            for i in range(nsig):
                v = sig_ref[(d * nsig + i) * slots + k]
                for block in blocks:
                    hit = hit | (v == block)
            list_ref[n] = d * stride + k
            return n + hit.astype(jnp.int32)

        return lax.fori_loop(0, live_ref[d], scan_slot, n)

    total = lax.fori_loop(0, live_ref.shape[0], scan_device, jnp.int32(0))
    for extra in range(3):
        list_ref[total + extra] = 0

    def blocks_of(row):
        d = row // stride
        return [sig_ref[(d * nsig + i) * slots + row - d * stride] for i in range(nsig)]

    def make(index, dst):
        row = list_ref[index]
        feats = point_terms(pts_ref, row)
        s = blocks_of(row)
        dst[...] = phi_rows(terms_ref, s, feats)

    def add(index, src):
        row = list_ref[index]
        valid = index < total
        s = blocks_of(row)
        wpot = wpot_ref[pl.ds(row, 1), :]
        cols = []
        for q in range(npiece):
            pos = jnp.int32(0)
            have = jnp.bool_(False)
            for i in range(nsig):
                eq = s[i] == blocks[q]
                pos = jnp.where(eq, i, pos)
                have = have | eq
            on = (have & valid).astype(jnp.float32)
            rows = src[pl.ds(pl.multiple_of(pos * BLOCK + offs[q], piece), piece), :]
            cols.append((rows.astype(jnp.float32) * (wpot * on)).astype(jnp.bfloat16))
        scaled = jnp.concatenate(cols, axis=0)
        delta = lax.dot_general(
            src[...], scaled, (((1,), (1,)), ((), ())), preferred_element_type=jnp.float32
        )
        for i in range(nsig):
            rows = pl.ds(pl.multiple_of(s[i] * BLOCK, BLOCK), BLOCK)
            out_ref[rows, :] += delta[i * BLOCK : (i + 1) * BLOCK]

    make(0, phi_a)

    def step(t, carry):
        make(2 * t + 1, phi_b)
        add(2 * t, phi_a)
        make(2 * t + 2, phi_a)
        add(2 * t + 1, phi_b)
        return carry

    lax.fori_loop(0, (total + 1) // 2, step, 0)


def shards(density, points, grid_weights, centres, exponents, sig_blocks, live_count):
    nrows = lax.axis_size("rows")
    ncols = lax.axis_size("cols")
    group = lax.axis_index("rows")
    col = lax.axis_index("cols")
    nsig = sig_blocks.shape[1]
    slots, _, npts = points.shape
    own_width = density.shape[0]
    span = own_width // BLOCK
    strip = own_width // ncols
    piece = math.gcd(strip, BLOCK)
    ratio = own_width // density.shape[1]
    nq = ncols // ratio
    stride = slots + 8
    held = span // ratio
    chunks = span * (2 if held % 2 == 0 and slots % (2 * span) == 0 else 1)

    vmem = pl.BlockSpec(memory_space=pltpu.VMEM)
    smem = pl.BlockSpec(memory_space=pltpu.SMEM)
    hbm = pl.BlockSpec(memory_space=pltpu.HBM)

    dma = pltpu.SemaphoreType.DMA
    pts_all, pot_all, energy, exc, terms = pl.pallas_call(
        functools.partial(exchange_kernel, nrows, ncols, nsig, chunks, stride),
        out_shape=(
            jax.ShapeDtypeStruct((3, ncols * stride, npts), jnp.float32),
            jax.ShapeDtypeStruct((ncols * stride, npts), jnp.float32),
            jax.ShapeDtypeStruct((slots, 1), jnp.float32),
            jax.ShapeDtypeStruct((8, BLOCK), jnp.float32),
            jax.ShapeDtypeStruct((span, BLOCK, 48), jnp.bfloat16),
        ),
        in_specs=[smem, smem, vmem, hbm, vmem, vmem, vmem, vmem],
        out_specs=(vmem, vmem, vmem, vmem, vmem),
        scratch_shapes=[
            pltpu.VMEM((span, span, BLOCK, BLOCK), jnp.bfloat16),
            pltpu.VMEM((slots * nsig * BLOCK, npts), jnp.bfloat16),
            pltpu.VMEM((slots, npts), jnp.float32),
            pltpu.VMEM((nrows, 8, BLOCK), jnp.float32),
            pltpu.VMEM((8, npts), jnp.float32),
            dma((span // ratio,)),
            dma((chunks,)),
            dma((chunks,)),
            dma((max(ratio - 1, 1), chunks)),
            dma((max(ratio - 1, 1), chunks)),
            dma((max(nq - 1, 1),)),
            dma((max(nq - 1, 1),)),
            dma((max(ratio - 1, 1), nq)),
            dma((max(ratio - 1, 1), nq)),
            dma((max(ncols - 1, 1),)),
            dma((max(ncols - 1, 1),)),
            dma((max(nrows - 1, 1),)),
            dma((max(nrows - 1, 1),)),
        ],
        compiler_params=pltpu.CompilerParams(
            collective_id=0, has_side_effects=True, vmem_limit_bytes=48 * 1024 * 1024
        ),
        name="exchange",
    )(
        sig_blocks.T, live_count, sig_blocks.T, density.reshape(span, BLOCK, -1), points.transpose(1, 0, 2),
        grid_weights, centres, exponents.reshape(1, -1),
    )
    own_energy = energy.reshape(slots)
    tails = pot_all.reshape(ncols, stride, npts)[:, slots : slots + 8]
    sig_all = (tails[:, 1 : 1 + nsig, :slots].astype(jnp.int32) - group * span).reshape(-1)
    live_all = tails[:, 1 + nsig, 0].astype(jnp.int32)

    xc_diag = pl.pallas_call(
        functools.partial(strip_kernel, nsig, slots, stride, piece),
        out_shape=jax.ShapeDtypeStruct((own_width, strip), jnp.float32),
        in_specs=[smem, smem, smem, vmem, vmem, vmem],
        out_specs=vmem,
        scratch_shapes=[
            pltpu.VMEM((nsig * BLOCK, npts), jnp.bfloat16),
            pltpu.VMEM((nsig * BLOCK, npts), jnp.bfloat16),
            pltpu.SMEM((ncols * slots + 8,), jnp.int32),
        ],
        compiler_params=pltpu.CompilerParams(vmem_limit_bytes=32 * 1024 * 1024),
        name="strip",
    )(sig_all, live_all, (col * strip).reshape(1).astype(jnp.int32), pts_all, pot_all, terms)
    return (xc_diag, own_energy, exc[0, 0])


def solution(mesh):
    placed = (
        P("rows", "cols"),
        P(("rows", "cols"), None, None),
        P(("rows", "cols"), None),
        P(),
        P(),
        P(("rows", "cols"), None),
        P(("rows", "cols")),
    )
    return jax.shard_map(
        shards,
        mesh=mesh,
        in_specs=placed,
        out_specs=(P("rows", "cols"), P(("rows", "cols")), P()),
        check_vma=False,
    )
```

```python
import functools
import math

import jax
import jax.numpy as jnp
from jax import lax
from jax.experimental import pallas as pl
from jax.experimental.pallas import tpu as pltpu
from jax.sharding import PartitionSpec as P

BLOCK = 128
slater = 0.7386


def function_terms(c, a):
    cc = c[0:1] * c[0:1] + c[1:2] * c[1:2] + c[2:3] * c[2:3]
    coef = jnp.concatenate([2.0 * a * c, -a, -a * cc, jnp.zeros_like(c)], axis=0)
    hi = coef.astype(jnp.bfloat16).astype(jnp.float32)
    rest = coef - hi
    mid = rest.astype(jnp.bfloat16).astype(jnp.float32)
    lo = rest - mid
    return jnp.concatenate([hi, mid, lo, hi, mid, hi], axis=0)


def point_terms(pts_ref, row):
    x, y, z = (pts_ref[axis, pl.ds(row, 1), :] for axis in range(3))
    r2 = x * x + y * y + z * z
    one = jnp.ones_like(x)
    zero = jnp.zeros_like(x)
    v = jnp.concatenate([x, y, z, r2, one, zero, zero, zero], axis=0)
    hi = v.astype(jnp.bfloat16).astype(jnp.float32)
    rest = v - hi
    mid = rest.astype(jnp.bfloat16).astype(jnp.float32)
    lo = rest - mid
    return jnp.concatenate([hi, hi, hi, mid, mid, lo], axis=0)


def phi_rows(terms_ref, s, feats):
    terms = jnp.concatenate([terms_ref[v] for v in s], axis=0)
    arg = jnp.dot(terms, feats, preferred_element_type=jnp.float32)
    return jnp.exp(arg).astype(jnp.bfloat16)


def exchange_kernel(
    nrows, ncols, nsig, chunks, stride,
    sig_ref, live_ref, sig_rows_ref, dens_ref, pts_ref, w_ref, centres_ref, expo_ref,
    pts_all_ref, pot_all_ref, energy_ref, exc_ref, terms_ref, terms_t_ref,
    diag_ref, phi_ref, rho_ref, ebuf_ref, meta_ref,
    local_sem, ring_send, ring_recv, sib_send, sib_recv,
    pts_send, pts_recv, fan_send, fan_recv, pot_send, pot_recv, pfan_send, pfan_recv, exc_send, exc_recv,
):
    group = lax.axis_index("rows")
    me = lax.axis_index("cols")
    slots, npts = w_ref.shape
    span = diag_ref.shape[0]
    held = dens_ref.shape[2] // BLOCK
    ratio = span // held
    nq = ncols // ratio
    lane, place = me % ratio, me // ratio

    def ring_of(q):
        return q // 2 * 2 + (q % 2 + q // 2) % 2 if nq % 2 == 0 else q

    direction = 1 - 2 * (lane % 2)
    ring = ring_of(place)
    after = ring_of((ring + direction + nq) % nq)
    dist = ((ring - ring_of(group)) * direction + 2 * nq) % nq

    barrier = pltpu.get_barrier_semaphore()
    for j in range(1, ncols):
        pl.semaphore_signal(
            barrier, inc=1, device_id=(group, (me + j) % ncols), device_id_type=pl.DeviceIdType.MESH
        )
    for j in range(1, nrows):
        pl.semaphore_signal(
            barrier, inc=1, device_id=((group + j) % nrows, me), device_id_type=pl.DeviceIdType.MESH
        )

    base = group * span
    for j in range(span):
        at = pl.ds(pl.multiple_of((base + j) * BLOCK, BLOCK), BLOCK)
        made = function_terms(centres_ref[:, at], expo_ref[:, at])
        terms_t_ref[j] = made.astype(jnp.bfloat16)
        terms_ref[j] = made.T.astype(jnp.bfloat16)
    live = live_ref[0].astype(jnp.float32)
    meta_ref[...] = jnp.zeros_like(meta_ref)
    meta_ref[1 : 1 + nsig, 0:slots] = sig_rows_ref[...].astype(jnp.float32)
    meta_ref[1 + nsig : 2 + nsig, :] = jnp.full((1, npts), live, jnp.float32)

    pl.semaphore_wait(barrier, ncols + nrows - 2)

    def remote(src, dst, send, recv, to_row, to_col):
        return pltpu.make_async_remote_copy(
            src_ref=src, dst_ref=dst, send_sem=send, recv_sem=recv,
            device_id=(to_row, to_col), device_id_type=pl.DeviceIdType.MESH,
        )

    @pl.when(dist == 0)
    def _():
        own = [
            pltpu.make_async_copy(
                dens_ref.at[:, :, pl.ds(j * BLOCK, BLOCK)], diag_ref.at[:, lane * held + j], local_sem.at[j]
            )
            for j in range(held)
        ]
        for copy in own:
            copy.start()
        for copy in own:
            copy.wait()

    cuts = chunks // span
    some = held // cuts

    def part(c, which):
        return diag_ref.at[c // cuts, pl.ds(which * held + c % cuts * some, some)]

    def ring_copy(c):
        return remote(part(c, lane), part(c, lane), ring_send.at[c], ring_recv.at[c], group, after * ratio + lane)

    def sib_copy(c, j, which):
        to = place * ratio + (lane + j) % ratio
        return remote(part(c, which), part(c, which), sib_send.at[j - 1, c], sib_recv.at[j - 1, c], group, to)

    per = slots // chunks
    mine = me * stride
    for axis in range(3):
        pts_all_ref[axis, pl.ds(pl.multiple_of(mine, 8), slots), :] = pts_ref[axis]

    def chunk_step(c, carry):
        @pl.when(dist > 0)
        def _():
            ring_copy(c).wait_recv()

        @pl.when(dist < nq - 1)
        def _():
            ring_copy(c).start()

        for j in range(1, ratio):
            sib_copy(c, j, lane).start()
        for u in range(per):
            k = c * per + u
            feats = point_terms(pts_ref, k).astype(jnp.bfloat16)
            s = [jnp.maximum(sig_ref[i, k] - base, 0) for i in range(nsig)]
            at = pl.multiple_of(k * nsig * BLOCK, nsig * BLOCK)
            phi_ref[pl.ds(at, nsig * BLOCK), :] = phi_rows(terms_ref, s, feats)
        return carry

    lax.fori_loop(0, chunks, chunk_step, 0)

    def slab(which):
        return pts_all_ref.at[:, pl.ds(pl.multiple_of(which * stride, 8), slots), :]

    def pts_copy(j, owner):
        to = (me + j * ratio) % ncols
        return remote(slab(owner), slab(owner), pts_send.at[j - 1], pts_recv.at[j - 1], group, to)

    def fan_copy(j, l, owner):
        to = place * ratio + (lane + l) % ratio
        return remote(slab(owner), slab(owner), fan_send.at[l - 1, j], fan_recv.at[l - 1, j], group, to)

    for j in range(1, nq):
        pts_copy(j, me).start()
    for l in range(1, ratio):
        fan_copy(0, l, me).start()

    def drain(c, carry):
        for j in range(1, ratio):
            sib_copy(c, j, (lane + ratio - j) % ratio).wait_recv()
        return carry

    lax.fori_loop(0, chunks, drain, 0)

    def image_rho(k):
        s = [jnp.maximum(sig_ref[i, k] - base, 0) for i in range(nsig)]
        phi = phi_ref[pl.ds(pl.multiple_of(k * nsig * BLOCK, BLOCK), nsig * BLOCK), :]
        dens = jnp.concatenate(
            [jnp.concatenate([diag_ref[s[i], s[j]] for j in range(nsig)], axis=1) for i in range(nsig)], axis=0
        )
        image = jnp.dot(dens, phi, preferred_element_type=jnp.float32)
        prod = phi.astype(jnp.float32) * image
        total = jnp.sum(prod.reshape(nsig * BLOCK // 8, 8, npts), axis=0)
        return jnp.sum(total, axis=0, keepdims=True)

    def image_step(t, carry):
        first = image_rho(2 * t)
        second = image_rho(2 * t + 1)
        rho_ref[pl.ds(2 * t, 1), :] = first
        rho_ref[pl.ds(2 * t + 1, 1), :] = second
        return carry

    half = slots // 4
    lax.fori_loop(0, half, image_step, 0)

    for j in range(1, nq):
        owner = (me + ncols - j * ratio) % ncols
        pts_copy(j, owner).wait_recv()
        for l in range(1, ratio):
            fan_copy(j, l, owner).start()

    lax.fori_loop(half, slots // 2, image_step, 0)

    slot = lax.broadcasted_iota(jnp.int32, (slots, npts), 0).astype(jnp.float32)
    w = w_ref[...] * jnp.clip(live - slot, 0.0, 1.0)
    rho = jnp.maximum(rho_ref[...], 0.0)
    above = rho > 0.0
    root = jnp.where(above, jnp.exp2(jnp.log2(jnp.where(above, rho, 1.0)) * (1.0 / 3.0)), 0.0)
    energy = jnp.sum(w * -slater * rho * root, axis=1, keepdims=True)
    energy_ref[...] = energy
    pot_all_ref[pl.ds(pl.multiple_of(mine, 8), slots), :] = (w * (-4.0 / 3.0 * slater)) * root
    own_sum = jnp.sum(energy, axis=0, keepdims=True)
    tail = lax.broadcasted_iota(jnp.int32, (8, npts), 0)
    pot_all_ref[pl.ds(pl.multiple_of(mine + slots, 8), 8), :] = jnp.where(
        tail == 0, jnp.broadcast_to(own_sum, (8, npts)), meta_ref[...]
    )

    def pot_slab(which):
        return pot_all_ref.at[pl.ds(pl.multiple_of(which * stride, 8), stride), :]

    def pot_copy(j, owner):
        to = (me + j * ratio) % ncols
        return remote(pot_slab(owner), pot_slab(owner), pot_send.at[j - 1], pot_recv.at[j - 1], group, to)

    def pfan_copy(j, l, owner):
        to = place * ratio + (lane + l) % ratio
        return remote(pot_slab(owner), pot_slab(owner), pfan_send.at[l - 1, j], pfan_recv.at[l - 1, j], group, to)

    for j in range(1, nq):
        pot_copy(j, me).start()
    for l in range(1, ratio):
        pfan_copy(0, l, me).start()

    def settle(c, carry):
        @pl.when(dist < nq - 1)
        def _():
            ring_copy(c).wait_send()

        for j in range(1, ratio):
            sib_copy(c, j, lane).wait_send()
        return carry

    lax.fori_loop(0, chunks, settle, 0)
    for j in range(1, nq):
        pts_copy(j, me).wait_send()
    for l in range(1, ratio):
        sibling = place * ratio + (lane + ratio - l) % ratio
        for j in range(nq):
            fan_copy(j, l, (me + ncols - j * ratio) % ncols).wait_send()
            fan_copy(j, l, (sibling + ncols - j * ratio) % ncols).wait_recv()
    for j in range(1, nq):
        owner = (me + ncols - j * ratio) % ncols
        pot_copy(j, owner).wait_recv()
        for l in range(1, ratio):
            pfan_copy(j, l, owner).start()
    for l in range(1, ratio):
        sibling = place * ratio + (lane + ratio - l) % ratio
        for j in range(nq):
            pfan_copy(j, l, (sibling + ncols - j * ratio) % ncols).wait_recv()

    part_sum = jnp.zeros((8, BLOCK), jnp.float32)
    for d in range(ncols):
        part_sum += pot_all_ref[d * stride + slots : d * stride + slots + 1, 0:BLOCK]
    ebuf_ref[group] = part_sum

    def exc_copy(j, owner):
        return remote(ebuf_ref.at[owner], ebuf_ref.at[owner], exc_send.at[j - 1], exc_recv.at[j - 1], (group + j) % nrows, me)

    for j in range(1, nrows):
        exc_copy(j, group).start()
    for j in range(1, nq):
        pot_copy(j, me).wait_send()
    for l in range(1, ratio):
        for j in range(nq):
            pfan_copy(j, l, (me + ncols - j * ratio) % ncols).wait_send()
    for j in range(1, nrows):
        exc_copy(j, (group + nrows - j) % nrows).wait_recv()
    exc = jnp.zeros((8, BLOCK), jnp.float32)
    for g in range(nrows):
        exc += ebuf_ref[g]
    exc_ref[...] = exc
    for j in range(1, nrows):
        exc_copy(j, group).wait_send()


def strip_kernel(nsig, slots, stride, piece, sig_ref, live_ref, col_ref, pts_ref, wpot_ref, terms_ref, terms_t_ref, out_ref, phi_a, phi_b, scaled_a, scaled_b, list_ref):
    strip = out_ref.shape[0]
    npiece = strip // piece
    start = col_ref[0]
    blocks = [(start + q * piece) // BLOCK for q in range(npiece)]
    out_ref[...] = jnp.zeros_like(out_ref)

    def scan_device(d, n):
        def scan_slot(k, n):
            hit = jnp.bool_(False)
            for i in range(nsig):
                v = sig_ref[(d * nsig + i) * slots + k]
                for block in blocks:
                    hit = hit | (v == block)
            list_ref[n] = d * stride + k
            return n + hit.astype(jnp.int32)

        return lax.fori_loop(0, live_ref[d], scan_slot, n)

    total = lax.fori_loop(0, live_ref.shape[0], scan_device, jnp.int32(0))
    for extra in range(3):
        list_ref[total + extra] = 0

    def blocks_of(row):
        d = row // stride
        return [sig_ref[(d * nsig + i) * slots + row - d * stride] for i in range(nsig)]

    own = terms_ref[pl.ds(pl.multiple_of(start, piece), strip), :]

    def make(index, phi_dst, scaled_dst):
        row = list_ref[index]
        valid = index < total
        feats = point_terms(pts_ref, row)
        s = blocks_of(row)
        terms = jnp.concatenate([terms_t_ref[v] for v in s], axis=1)
        arg = jnp.dot(feats.T.astype(jnp.bfloat16), terms, preferred_element_type=jnp.float32)
        phi_dst[...] = jnp.exp(arg).astype(jnp.bfloat16)
        wpot = wpot_ref[pl.ds(row, 1), :]
        arg = jnp.dot(own, feats.astype(jnp.bfloat16), preferred_element_type=jnp.float32)
        phi = jnp.exp(arg).astype(jnp.bfloat16).astype(jnp.float32)
        for q in range(npiece):
            have = jnp.bool_(False)
            for v in s:
                have = have | (v == blocks[q])
            on = (have & valid).astype(jnp.float32)
            rows = phi[q * piece : (q + 1) * piece] * (wpot * on)
            scaled_dst[pl.ds(q * piece, piece), :] = rows.astype(jnp.bfloat16)

    def add(index, phi_src, scaled_src):
        s = blocks_of(list_ref[index])
        delta = jnp.dot(scaled_src[...], phi_src[...], preferred_element_type=jnp.float32)
        for i in range(nsig):
            cols = pl.ds(pl.multiple_of(s[i] * BLOCK, BLOCK), BLOCK)
            out_ref[:, cols] += delta[:, i * BLOCK : (i + 1) * BLOCK]

    make(0, phi_a, scaled_a)

    def step(t, carry):
        make(2 * t + 1, phi_b, scaled_b)
        add(2 * t, phi_a, scaled_a)
        make(2 * t + 2, phi_a, scaled_a)
        add(2 * t + 1, phi_b, scaled_b)
        return carry

    lax.fori_loop(0, (total + 1) // 2, step, 0)


def shards(density, points, grid_weights, centres, exponents, sig_blocks, live_count):
    nrows = lax.axis_size("rows")
    ncols = lax.axis_size("cols")
    group = lax.axis_index("rows")
    col = lax.axis_index("cols")
    nsig = sig_blocks.shape[1]
    slots, _, npts = points.shape
    own_width = density.shape[0]
    span = own_width // BLOCK
    strip = own_width // ncols
    piece = math.gcd(strip, BLOCK)
    ratio = own_width // density.shape[1]
    nq = ncols // ratio
    stride = slots + 8
    held = span // ratio
    chunks = span * (2 if held % 2 == 0 and slots % (2 * span) == 0 else 1)

    vmem = pl.BlockSpec(memory_space=pltpu.VMEM)
    smem = pl.BlockSpec(memory_space=pltpu.SMEM)
    hbm = pl.BlockSpec(memory_space=pltpu.HBM)

    dma = pltpu.SemaphoreType.DMA
    pts_all, pot_all, energy, exc, terms, terms_t = pl.pallas_call(
        functools.partial(exchange_kernel, nrows, ncols, nsig, chunks, stride),
        out_shape=(
            jax.ShapeDtypeStruct((3, ncols * stride, npts), jnp.float32),
            jax.ShapeDtypeStruct((ncols * stride, npts), jnp.float32),
            jax.ShapeDtypeStruct((slots, 1), jnp.float32),
            jax.ShapeDtypeStruct((8, BLOCK), jnp.float32),
            jax.ShapeDtypeStruct((span, BLOCK, 48), jnp.bfloat16),
            jax.ShapeDtypeStruct((span, 48, BLOCK), jnp.bfloat16),
        ),
        in_specs=[smem, smem, vmem, hbm, vmem, vmem, vmem, vmem],
        out_specs=(vmem,) * 6,
        scratch_shapes=[
            pltpu.VMEM((span, span, BLOCK, BLOCK), jnp.bfloat16),
            pltpu.VMEM((slots * nsig * BLOCK, npts), jnp.bfloat16),
            pltpu.VMEM((slots, npts), jnp.float32),
            pltpu.VMEM((nrows, 8, BLOCK), jnp.float32),
            pltpu.VMEM((8, npts), jnp.float32),
            dma((span // ratio,)),
            dma((chunks,)),
            dma((chunks,)),
            dma((max(ratio - 1, 1), chunks)),
            dma((max(ratio - 1, 1), chunks)),
            dma((max(nq - 1, 1),)),
            dma((max(nq - 1, 1),)),
            dma((max(ratio - 1, 1), nq)),
            dma((max(ratio - 1, 1), nq)),
            dma((max(nq - 1, 1),)),
            dma((max(nq - 1, 1),)),
            dma((max(ratio - 1, 1), nq)),
            dma((max(ratio - 1, 1), nq)),
            dma((max(nrows - 1, 1),)),
            dma((max(nrows - 1, 1),)),
        ],
        compiler_params=pltpu.CompilerParams(
            collective_id=0, has_side_effects=True, vmem_limit_bytes=48 * 1024 * 1024
        ),
        name="exchange",
    )(
        sig_blocks.T, live_count, sig_blocks.T, density.reshape(span, BLOCK, -1), points.transpose(1, 0, 2),
        grid_weights, centres, exponents.reshape(1, -1),
    )
    own_energy = energy.reshape(slots)
    tails = pot_all.reshape(ncols, stride, npts)[:, slots : slots + 8]
    sig_all = (tails[:, 1 : 1 + nsig, :slots].astype(jnp.int32) - group * span).reshape(-1)
    live_all = tails[:, 1 + nsig, 0].astype(jnp.int32)

    xc_strip = pl.pallas_call(
        functools.partial(strip_kernel, nsig, slots, stride, piece),
        out_shape=jax.ShapeDtypeStruct((strip, own_width), jnp.float32),
        in_specs=[smem, smem, smem, vmem, vmem, vmem, vmem],
        out_specs=vmem,
        scratch_shapes=[
            pltpu.VMEM((npts, nsig * BLOCK), jnp.bfloat16),
            pltpu.VMEM((npts, nsig * BLOCK), jnp.bfloat16),
            pltpu.VMEM((strip, npts), jnp.bfloat16),
            pltpu.VMEM((strip, npts), jnp.bfloat16),
            pltpu.SMEM((ncols * slots + 8,), jnp.int32),
        ],
        compiler_params=pltpu.CompilerParams(vmem_limit_bytes=32 * 1024 * 1024),
        name="strip",
    )(sig_all, live_all, (col * strip).reshape(1).astype(jnp.int32), pts_all, pot_all, terms.reshape(own_width, -1), terms_t)
    return (xc_strip.T, own_energy, exc[0, 0])


def solution(mesh):
    placed = (
        P("rows", "cols"),
        P(("rows", "cols"), None, None),
        P(("rows", "cols"), None),
        P(),
        P(),
        P(("rows", "cols"), None),
        P(("rows", "cols")),
    )
    return jax.shard_map(
        shards,
        mesh=mesh,
        in_specs=placed,
        out_specs=(P("rows", "cols"), P(("rows", "cols")), P()),
        check_vma=False,
    )
```

```python
import functools
import math

import jax
import jax.numpy as jnp
from jax import lax
from jax.experimental import pallas as pl
from jax.experimental.pallas import tpu as pltpu
from jax.sharding import PartitionSpec as P

BLOCK = 128
slater = 0.7386


def function_terms(c, a):
    cc = c[0:1] * c[0:1] + c[1:2] * c[1:2] + c[2:3] * c[2:3]
    coef = jnp.concatenate([2.0 * a * c, -a, -a * cc, jnp.zeros_like(c)], axis=0)
    hi = coef.astype(jnp.bfloat16).astype(jnp.float32)
    rest = coef - hi
    mid = rest.astype(jnp.bfloat16).astype(jnp.float32)
    lo = rest - mid
    return jnp.concatenate([hi, mid, lo, hi, mid, hi], axis=0)


def point_terms(pts_ref, row):
    x, y, z = (pts_ref[axis, pl.ds(row, 1), :] for axis in range(3))
    r2 = x * x + y * y + z * z
    one = jnp.ones_like(x)
    zero = jnp.zeros_like(x)
    v = jnp.concatenate([x, y, z, r2, one, zero, zero, zero], axis=0)
    hi = v.astype(jnp.bfloat16).astype(jnp.float32)
    rest = v - hi
    mid = rest.astype(jnp.bfloat16).astype(jnp.float32)
    lo = rest - mid
    return jnp.concatenate([hi, hi, hi, mid, mid, lo], axis=0)


def phi_rows(terms_ref, s, feats):
    terms = jnp.concatenate([terms_ref[v] for v in s], axis=0)
    arg = jnp.dot(terms, feats, preferred_element_type=jnp.float32)
    return jnp.exp(arg).astype(jnp.bfloat16)


def exchange_kernel(
    nrows, ncols, nsig, chunks, stride,
    sig_ref, live_ref, sig_rows_ref, dens_ref, pts_ref, w_ref, centres_ref, expo_ref,
    pts_all_ref, pot_all_ref, energy_ref, exc_ref, terms_ref, terms_t_ref,
    diag_ref, phi_ref, rho_ref, ebuf_ref, meta_ref,
    local_sem, ring_send, ring_recv, sib_send, sib_recv,
    pts_send, pts_recv, fan_send, fan_recv, pot_send, pot_recv, pfan_send, pfan_recv, exc_send, exc_recv,
):
    group = lax.axis_index("rows")
    me = lax.axis_index("cols")
    slots, npts = w_ref.shape
    span = diag_ref.shape[0]
    held = dens_ref.shape[2] // BLOCK
    ratio = span // held
    nq = ncols // ratio
    lane, place = me % ratio, me // ratio

    def ring_of(q):
        return q // 2 * 2 + (q % 2 + q // 2) % 2 if nq % 2 == 0 else q

    ring = ring_of(place)

    def after(c):
        return ring_of((ring + 1 - 2 * (c % 2) + nq) % nq)

    def dist(c):
        return ((ring - ring_of(group)) * (1 - 2 * (c % 2)) + 2 * nq) % nq

    barrier = pltpu.get_barrier_semaphore()
    for j in range(1, ncols):
        pl.semaphore_signal(
            barrier, inc=1, device_id=(group, (me + j) % ncols), device_id_type=pl.DeviceIdType.MESH
        )
    for j in range(1, nrows):
        pl.semaphore_signal(
            barrier, inc=1, device_id=((group + j) % nrows, me), device_id_type=pl.DeviceIdType.MESH
        )

    base = group * span
    for j in range(span):
        at = pl.ds(pl.multiple_of((base + j) * BLOCK, BLOCK), BLOCK)
        made = function_terms(centres_ref[:, at], expo_ref[:, at])
        terms_t_ref[j] = made.astype(jnp.bfloat16)
        terms_ref[j] = made.T.astype(jnp.bfloat16)
    live = live_ref[0].astype(jnp.float32)
    meta_ref[...] = jnp.zeros_like(meta_ref)
    meta_ref[1 : 1 + nsig, 0:slots] = sig_rows_ref[...].astype(jnp.float32)
    meta_ref[1 + nsig : 2 + nsig, :] = jnp.full((1, npts), live, jnp.float32)

    pl.semaphore_wait(barrier, ncols + nrows - 2)

    def remote(src, dst, send, recv, to_row, to_col):
        return pltpu.make_async_remote_copy(
            src_ref=src, dst_ref=dst, send_sem=send, recv_sem=recv,
            device_id=(to_row, to_col), device_id_type=pl.DeviceIdType.MESH,
        )

    @pl.when(ring == ring_of(group))
    def _():
        own = [
            pltpu.make_async_copy(
                dens_ref.at[:, :, pl.ds(j * BLOCK, BLOCK)], diag_ref.at[:, lane * held + j], local_sem.at[j]
            )
            for j in range(held)
        ]
        for copy in own:
            copy.start()
        for copy in own:
            copy.wait()

    cuts = chunks // span
    some = held // cuts

    def part(c, which):
        return diag_ref.at[c // cuts, pl.ds(which * held + c % cuts * some, some)]

    def ring_copy(c):
        return remote(part(c, lane), part(c, lane), ring_send.at[c], ring_recv.at[c], group, after(c) * ratio + lane)

    def sib_copy(c, j, which):
        to = place * ratio + (lane + j) % ratio
        return remote(part(c, which), part(c, which), sib_send.at[j - 1, c], sib_recv.at[j - 1, c], group, to)

    per = slots // chunks
    mine = me * stride
    for axis in range(3):
        pts_all_ref[axis, pl.ds(pl.multiple_of(mine, 8), slots), :] = pts_ref[axis]

    def chunk_step(c, carry):
        @pl.when(dist(c) > 0)
        def _():
            ring_copy(c).wait_recv()

        @pl.when(dist(c) < nq - 1)
        def _():
            ring_copy(c).start()

        for j in range(1, ratio):
            sib_copy(c, j, lane).start()
        for u in range(per):
            k = c * per + u
            feats = point_terms(pts_ref, k).astype(jnp.bfloat16)
            s = [jnp.maximum(sig_ref[i, k] - base, 0) for i in range(nsig)]
            at = pl.multiple_of(k * nsig * BLOCK, nsig * BLOCK)
            phi_ref[pl.ds(at, nsig * BLOCK), :] = phi_rows(terms_ref, s, feats)
        return carry

    lax.fori_loop(0, chunks, chunk_step, 0)

    def slab(which):
        return pts_all_ref.at[:, pl.ds(pl.multiple_of(which * stride, 8), slots), :]

    def pts_copy(j, owner):
        to = (me + j * ratio) % ncols
        return remote(slab(owner), slab(owner), pts_send.at[j - 1], pts_recv.at[j - 1], group, to)

    def fan_copy(j, l, owner):
        to = place * ratio + (lane + l) % ratio
        return remote(slab(owner), slab(owner), fan_send.at[l - 1, j], fan_recv.at[l - 1, j], group, to)

    for j in range(1, nq):
        pts_copy(j, me).start()
    for l in range(1, ratio):
        fan_copy(0, l, me).start()

    def drain(c, carry):
        for j in range(1, ratio):
            sib_copy(c, j, (lane + ratio - j) % ratio).wait_recv()
        return carry

    lax.fori_loop(0, chunks, drain, 0)

    def image_rho(k):
        s = [jnp.maximum(sig_ref[i, k] - base, 0) for i in range(nsig)]
        phi = phi_ref[pl.ds(pl.multiple_of(k * nsig * BLOCK, BLOCK), nsig * BLOCK), :]
        dens = jnp.concatenate(
            [jnp.concatenate([diag_ref[s[i], s[j]] for j in range(nsig)], axis=1) for i in range(nsig)], axis=0
        )
        image = jnp.dot(dens, phi, preferred_element_type=jnp.float32)
        prod = phi.astype(jnp.float32) * image
        total = jnp.sum(prod.reshape(nsig * BLOCK // 8, 8, npts), axis=0)
        return jnp.sum(total, axis=0, keepdims=True)

    def image_step(t, carry):
        first = image_rho(2 * t)
        second = image_rho(2 * t + 1)
        rho_ref[pl.ds(2 * t, 1), :] = first
        rho_ref[pl.ds(2 * t + 1, 1), :] = second
        return carry

    half = slots // 4
    lax.fori_loop(0, half, image_step, 0)

    for j in range(1, nq):
        owner = (me + ncols - j * ratio) % ncols
        pts_copy(j, owner).wait_recv()
        for l in range(1, ratio):
            fan_copy(j, l, owner).start()

    lax.fori_loop(half, slots // 2, image_step, 0)

    slot = lax.broadcasted_iota(jnp.int32, (slots, npts), 0).astype(jnp.float32)
    w = w_ref[...] * jnp.clip(live - slot, 0.0, 1.0)
    rho = jnp.maximum(rho_ref[...], 0.0)
    above = rho > 0.0
    root = jnp.where(above, jnp.exp2(jnp.log2(jnp.where(above, rho, 1.0)) * (1.0 / 3.0)), 0.0)
    energy = jnp.sum(w * -slater * rho * root, axis=1, keepdims=True)
    energy_ref[...] = energy
    pot_all_ref[pl.ds(pl.multiple_of(mine, 8), slots), :] = (w * (-4.0 / 3.0 * slater)) * root
    own_sum = jnp.sum(energy, axis=0, keepdims=True)
    tail = lax.broadcasted_iota(jnp.int32, (8, npts), 0)
    pot_all_ref[pl.ds(pl.multiple_of(mine + slots, 8), 8), :] = jnp.where(
        tail == 0, jnp.broadcast_to(own_sum, (8, npts)), meta_ref[...]
    )

    def pot_slab(which):
        return pot_all_ref.at[pl.ds(pl.multiple_of(which * stride, 8), stride), :]

    def pot_copy(j, owner):
        to = (me + j * ratio) % ncols
        return remote(pot_slab(owner), pot_slab(owner), pot_send.at[j - 1], pot_recv.at[j - 1], group, to)

    def pfan_copy(j, l, owner):
        to = place * ratio + (lane + l) % ratio
        return remote(pot_slab(owner), pot_slab(owner), pfan_send.at[l - 1, j], pfan_recv.at[l - 1, j], group, to)

    for j in range(1, nq):
        pot_copy(j, me).start()
    for l in range(1, ratio):
        pfan_copy(0, l, me).start()

    def settle(c, carry):
        @pl.when(dist(c) < nq - 1)
        def _():
            ring_copy(c).wait_send()

        for j in range(1, ratio):
            sib_copy(c, j, lane).wait_send()
        return carry

    lax.fori_loop(0, chunks, settle, 0)
    for j in range(1, nq):
        pts_copy(j, me).wait_send()
    for l in range(1, ratio):
        sibling = place * ratio + (lane + ratio - l) % ratio
        for j in range(nq):
            fan_copy(j, l, (me + ncols - j * ratio) % ncols).wait_send()
            fan_copy(j, l, (sibling + ncols - j * ratio) % ncols).wait_recv()
    for j in range(1, nq):
        owner = (me + ncols - j * ratio) % ncols
        pot_copy(j, owner).wait_recv()
        for l in range(1, ratio):
            pfan_copy(j, l, owner).start()
    for l in range(1, ratio):
        sibling = place * ratio + (lane + ratio - l) % ratio
        for j in range(nq):
            pfan_copy(j, l, (sibling + ncols - j * ratio) % ncols).wait_recv()

    part_sum = jnp.zeros((8, BLOCK), jnp.float32)
    for d in range(ncols):
        part_sum += pot_all_ref[d * stride + slots : d * stride + slots + 1, 0:BLOCK]
    ebuf_ref[group] = part_sum

    def exc_copy(j, owner):
        return remote(ebuf_ref.at[owner], ebuf_ref.at[owner], exc_send.at[j - 1], exc_recv.at[j - 1], (group + j) % nrows, me)

    for j in range(1, nrows):
        exc_copy(j, group).start()
    for j in range(1, nq):
        pot_copy(j, me).wait_send()
    for l in range(1, ratio):
        for j in range(nq):
            pfan_copy(j, l, (me + ncols - j * ratio) % ncols).wait_send()
    for j in range(1, nrows):
        exc_copy(j, (group + nrows - j) % nrows).wait_recv()
    exc = jnp.zeros((8, BLOCK), jnp.float32)
    for g in range(nrows):
        exc += ebuf_ref[g]
    exc_ref[...] = exc
    for j in range(1, nrows):
        exc_copy(j, group).wait_send()


def strip_kernel(nsig, slots, stride, piece, sig_ref, live_ref, col_ref, pts_ref, wpot_ref, terms_ref, terms_t_ref, out_ref, phi_a, phi_b, scaled_a, scaled_b, list_ref):
    strip = out_ref.shape[0]
    npiece = strip // piece
    start = col_ref[0]
    blocks = [(start + q * piece) // BLOCK for q in range(npiece)]
    out_ref[...] = jnp.zeros_like(out_ref)

    def scan_device(d, n):
        def scan_slot(k, n):
            hit = jnp.bool_(False)
            for i in range(nsig):
                v = sig_ref[(d * nsig + i) * slots + k]
                for block in blocks:
                    hit = hit | (v == block)
            list_ref[n] = d * stride + k
            return n + hit.astype(jnp.int32)

        return lax.fori_loop(0, live_ref[d], scan_slot, n)

    total = lax.fori_loop(0, live_ref.shape[0], scan_device, jnp.int32(0))
    for extra in range(3):
        list_ref[total + extra] = 0

    def blocks_of(row):
        d = row // stride
        return [sig_ref[(d * nsig + i) * slots + row - d * stride] for i in range(nsig)]

    own = terms_ref[pl.ds(pl.multiple_of(start, piece), strip), :]

    def make(index, phi_dst, scaled_dst):
        row = list_ref[index]
        valid = index < total
        feats = point_terms(pts_ref, row)
        s = blocks_of(row)
        terms = jnp.concatenate([terms_t_ref[v] for v in s], axis=1)
        arg = jnp.dot(feats.T.astype(jnp.bfloat16), terms, preferred_element_type=jnp.float32)
        phi_dst[...] = jnp.exp(arg).astype(jnp.bfloat16)
        wpot = wpot_ref[pl.ds(row, 1), :]
        arg = jnp.dot(own, feats.astype(jnp.bfloat16), preferred_element_type=jnp.float32)
        phi = jnp.exp(arg).astype(jnp.bfloat16).astype(jnp.float32)
        for q in range(npiece):
            have = jnp.bool_(False)
            for v in s:
                have = have | (v == blocks[q])
            on = (have & valid).astype(jnp.float32)
            rows = phi[q * piece : (q + 1) * piece] * (wpot * on)
            scaled_dst[pl.ds(q * piece, piece), :] = rows.astype(jnp.bfloat16)

    def add(index, phi_src, scaled_src):
        s = blocks_of(list_ref[index])
        delta = jnp.dot(scaled_src[...], phi_src[...], preferred_element_type=jnp.float32)
        for i in range(nsig):
            cols = pl.ds(pl.multiple_of(s[i] * BLOCK, BLOCK), BLOCK)
            out_ref[:, cols] += delta[:, i * BLOCK : (i + 1) * BLOCK]

    make(0, phi_a, scaled_a)

    def step(t, carry):
        make(2 * t + 1, phi_b, scaled_b)
        add(2 * t, phi_a, scaled_a)
        make(2 * t + 2, phi_a, scaled_a)
        add(2 * t + 1, phi_b, scaled_b)
        return carry

    lax.fori_loop(0, (total + 1) // 2, step, 0)


def shards(density, points, grid_weights, centres, exponents, sig_blocks, live_count):
    nrows = lax.axis_size("rows")
    ncols = lax.axis_size("cols")
    group = lax.axis_index("rows")
    col = lax.axis_index("cols")
    nsig = sig_blocks.shape[1]
    slots, _, npts = points.shape
    own_width = density.shape[0]
    span = own_width // BLOCK
    strip = own_width // ncols
    piece = math.gcd(strip, BLOCK)
    ratio = own_width // density.shape[1]
    nq = ncols // ratio
    stride = slots + 8
    held = span // ratio
    chunks = span * (2 if held % 2 == 0 and slots % (2 * span) == 0 else 1)

    vmem = pl.BlockSpec(memory_space=pltpu.VMEM)
    smem = pl.BlockSpec(memory_space=pltpu.SMEM)
    hbm = pl.BlockSpec(memory_space=pltpu.HBM)

    dma = pltpu.SemaphoreType.DMA
    pts_all, pot_all, energy, exc, terms, terms_t = pl.pallas_call(
        functools.partial(exchange_kernel, nrows, ncols, nsig, chunks, stride),
        out_shape=(
            jax.ShapeDtypeStruct((3, ncols * stride, npts), jnp.float32),
            jax.ShapeDtypeStruct((ncols * stride, npts), jnp.float32),
            jax.ShapeDtypeStruct((slots, 1), jnp.float32),
            jax.ShapeDtypeStruct((8, BLOCK), jnp.float32),
            jax.ShapeDtypeStruct((span, BLOCK, 48), jnp.bfloat16),
            jax.ShapeDtypeStruct((span, 48, BLOCK), jnp.bfloat16),
        ),
        in_specs=[smem, smem, vmem, hbm, vmem, vmem, vmem, vmem],
        out_specs=(vmem,) * 6,
        scratch_shapes=[
            pltpu.VMEM((span, span, BLOCK, BLOCK), jnp.bfloat16),
            pltpu.VMEM((slots * nsig * BLOCK, npts), jnp.bfloat16),
            pltpu.VMEM((slots, npts), jnp.float32),
            pltpu.VMEM((nrows, 8, BLOCK), jnp.float32),
            pltpu.VMEM((8, npts), jnp.float32),
            dma((span // ratio,)),
            dma((chunks,)),
            dma((chunks,)),
            dma((max(ratio - 1, 1), chunks)),
            dma((max(ratio - 1, 1), chunks)),
            dma((max(nq - 1, 1),)),
            dma((max(nq - 1, 1),)),
            dma((max(ratio - 1, 1), nq)),
            dma((max(ratio - 1, 1), nq)),
            dma((max(nq - 1, 1),)),
            dma((max(nq - 1, 1),)),
            dma((max(ratio - 1, 1), nq)),
            dma((max(ratio - 1, 1), nq)),
            dma((max(nrows - 1, 1),)),
            dma((max(nrows - 1, 1),)),
        ],
        compiler_params=pltpu.CompilerParams(
            collective_id=0, has_side_effects=True, vmem_limit_bytes=48 * 1024 * 1024
        ),
        name="exchange",
    )(
        sig_blocks.T, live_count, sig_blocks.T, density.reshape(span, BLOCK, -1), points.transpose(1, 0, 2),
        grid_weights, centres, exponents.reshape(1, -1),
    )
    own_energy = energy.reshape(slots)
    tails = pot_all.reshape(ncols, stride, npts)[:, slots : slots + 8]
    sig_all = (tails[:, 1 : 1 + nsig, :slots].astype(jnp.int32) - group * span).reshape(-1)
    live_all = tails[:, 1 + nsig, 0].astype(jnp.int32)

    xc_strip = pl.pallas_call(
        functools.partial(strip_kernel, nsig, slots, stride, piece),
        out_shape=jax.ShapeDtypeStruct((strip, own_width), jnp.float32),
        in_specs=[smem, smem, smem, vmem, vmem, vmem, vmem],
        out_specs=vmem,
        scratch_shapes=[
            pltpu.VMEM((npts, nsig * BLOCK), jnp.bfloat16),
            pltpu.VMEM((npts, nsig * BLOCK), jnp.bfloat16),
            pltpu.VMEM((strip, npts), jnp.bfloat16),
            pltpu.VMEM((strip, npts), jnp.bfloat16),
            pltpu.SMEM((ncols * slots + 8,), jnp.int32),
        ],
        compiler_params=pltpu.CompilerParams(vmem_limit_bytes=32 * 1024 * 1024),
        name="strip",
    )(sig_all, live_all, (col * strip).reshape(1).astype(jnp.int32), pts_all, pot_all, terms.reshape(own_width, -1), terms_t)
    return (xc_strip.T, own_energy, exc[0, 0])


def solution(mesh):
    placed = (
        P("rows", "cols"),
        P(("rows", "cols"), None, None),
        P(("rows", "cols"), None),
        P(),
        P(),
        P(("rows", "cols"), None),
        P(("rows", "cols")),
    )
    return jax.shard_map(
        shards,
        mesh=mesh,
        in_specs=placed,
        out_specs=(P("rows", "cols"), P(("rows", "cols")), P()),
        check_vma=False,
    )
```

```python
import functools
import math

import jax
import jax.numpy as jnp
from jax import lax
from jax.experimental import pallas as pl
from jax.experimental.pallas import tpu as pltpu
from jax.sharding import PartitionSpec as P

BLOCK = 128
slater = 0.7386


def function_terms(c, a):
    cc = c[0:1] * c[0:1] + c[1:2] * c[1:2] + c[2:3] * c[2:3]
    coef = jnp.concatenate([2.0 * a * c, -a, -a * cc, jnp.zeros_like(c)], axis=0)
    hi = coef.astype(jnp.bfloat16).astype(jnp.float32)
    rest = coef - hi
    mid = rest.astype(jnp.bfloat16).astype(jnp.float32)
    lo = rest - mid
    return jnp.concatenate([hi, mid, lo, hi, mid, hi], axis=0)


def point_terms(pts_ref, row):
    x, y, z = (pts_ref[axis, pl.ds(row, 1), :] for axis in range(3))
    r2 = x * x + y * y + z * z
    one = jnp.ones_like(x)
    zero = jnp.zeros_like(x)
    v = jnp.concatenate([x, y, z, r2, one, zero, zero, zero], axis=0)
    hi = v.astype(jnp.bfloat16).astype(jnp.float32)
    rest = v - hi
    mid = rest.astype(jnp.bfloat16).astype(jnp.float32)
    lo = rest - mid
    return jnp.concatenate([hi, hi, hi, mid, mid, lo], axis=0)


def phi_rows(terms_ref, s, feats):
    terms = jnp.concatenate([terms_ref[v] for v in s], axis=0)
    arg = jnp.dot(terms, feats, preferred_element_type=jnp.float32)
    return jnp.exp(arg).astype(jnp.bfloat16)


def exchange_kernel(
    nrows, ncols, nsig, chunks, stride,
    sig_ref, live_ref, sig_rows_ref, dens_ref, pts_ref, w_ref, centres_ref, expo_ref,
    pts_all_ref, pot_all_ref, energy_ref, exc_ref, terms_ref, terms_t_ref,
    diag_ref, phi_ref, rho_ref, ebuf_ref, meta_ref,
    local_sem, ring_send, ring_recv, sib_send, sib_recv,
    pts_send, pts_recv, fan_send, fan_recv, pot_send, pot_recv, pfan_send, pfan_recv, exc_send, exc_recv,
):
    group = lax.axis_index("rows")
    me = lax.axis_index("cols")
    slots, npts = w_ref.shape
    span = diag_ref.shape[0]
    held = dens_ref.shape[2] // BLOCK
    ratio = span // held
    nq = ncols // ratio
    lane, place = me % ratio, me // ratio

    def ring_of(q):
        return q // 2 * 2 + (q % 2 + q // 2) % 2 if nq % 2 == 0 else q

    ring = ring_of(place)

    def after(c):
        return ring_of((ring + 1 - 2 * (c % 2) + nq) % nq)

    def dist(c):
        return ((ring - ring_of(group)) * (1 - 2 * (c % 2)) + 2 * nq) % nq

    barrier = pltpu.get_barrier_semaphore()
    for j in range(1, ncols):
        pl.semaphore_signal(
            barrier, inc=1, device_id=(group, (me + j) % ncols), device_id_type=pl.DeviceIdType.MESH
        )
    for j in range(1, nrows):
        pl.semaphore_signal(
            barrier, inc=1, device_id=((group + j) % nrows, me), device_id_type=pl.DeviceIdType.MESH
        )

    base = group * span
    for j in range(span):
        at = pl.ds(pl.multiple_of((base + j) * BLOCK, BLOCK), BLOCK)
        made = function_terms(centres_ref[:, at], expo_ref[:, at])
        terms_t_ref[j] = made.astype(jnp.bfloat16)
        terms_ref[j] = made.T.astype(jnp.bfloat16)
    live = live_ref[0].astype(jnp.float32)
    meta_ref[...] = jnp.zeros_like(meta_ref)
    meta_ref[1 : 1 + nsig, 0:slots] = sig_rows_ref[...].astype(jnp.float32)
    meta_ref[1 + nsig : 2 + nsig, :] = jnp.full((1, npts), live, jnp.float32)

    pl.semaphore_wait(barrier, ncols + nrows - 2)

    def remote(src, dst, send, recv, to_row, to_col):
        return pltpu.make_async_remote_copy(
            src_ref=src, dst_ref=dst, send_sem=send, recv_sem=recv,
            device_id=(to_row, to_col), device_id_type=pl.DeviceIdType.MESH,
        )

    @pl.when(ring == ring_of(group))
    def _():
        own = [
            pltpu.make_async_copy(
                dens_ref.at[:, :, pl.ds(j * BLOCK, BLOCK)], diag_ref.at[:, lane * held + j], local_sem.at[j]
            )
            for j in range(held)
        ]
        for copy in own:
            copy.start()
        for copy in own:
            copy.wait()

    cuts = chunks // span
    some = held // cuts

    def part(c, which):
        return diag_ref.at[c // cuts, pl.ds(which * held + c % cuts * some, some)]

    def ring_copy(c):
        return remote(part(c, lane), part(c, lane), ring_send.at[c], ring_recv.at[c], group, after(c) * ratio + lane)

    def sib_copy(c, j, which):
        to = place * ratio + (lane + j) % ratio
        return remote(part(c, which), part(c, which), sib_send.at[j - 1, c], sib_recv.at[j - 1, c], group, to)

    steps = chunks // 2
    per = slots // steps
    mine = me * stride
    for axis in range(3):
        pts_all_ref[axis, pl.ds(pl.multiple_of(mine, 8), slots), :] = pts_ref[axis]

    def move(t, e):
        c = 2 * (t - dist(e)) + e

        @pl.when((c >= 0) & (c < chunks))
        def _():
            @pl.when(dist(e) > 0)
            def _():
                ring_copy(c).wait_recv()

            @pl.when(dist(e) < nq - 1)
            def _():
                ring_copy(c).start()

            for j in range(1, ratio):
                sib_copy(c, j, lane).start()

    def late_step(t, carry):
        move(t, 0)
        move(t, 1)
        return carry

    def chunk_step(t, carry):
        late_step(t, carry)
        for u in range(per):
            k = t * per + u
            feats = point_terms(pts_ref, k).astype(jnp.bfloat16)
            s = [jnp.maximum(sig_ref[i, k] - base, 0) for i in range(nsig)]
            at = pl.multiple_of(k * nsig * BLOCK, nsig * BLOCK)
            phi_ref[pl.ds(at, nsig * BLOCK), :] = phi_rows(terms_ref, s, feats)
        return carry

    lax.fori_loop(0, steps, chunk_step, 0)
    lax.fori_loop(steps, steps + nq - 1, late_step, 0)

    def slab(which):
        return pts_all_ref.at[:, pl.ds(pl.multiple_of(which * stride, 8), slots), :]

    def pts_copy(j, owner):
        to = (me + j * ratio) % ncols
        return remote(slab(owner), slab(owner), pts_send.at[j - 1], pts_recv.at[j - 1], group, to)

    def fan_copy(j, l, owner):
        to = place * ratio + (lane + l) % ratio
        return remote(slab(owner), slab(owner), fan_send.at[l - 1, j], fan_recv.at[l - 1, j], group, to)

    for j in range(1, nq):
        pts_copy(j, me).start()
    for l in range(1, ratio):
        fan_copy(0, l, me).start()

    def drain(c, carry):
        for j in range(1, ratio):
            sib_copy(c, j, (lane + ratio - j) % ratio).wait_recv()
        return carry

    lax.fori_loop(0, chunks, drain, 0)

    def image_rho(k):
        s = [jnp.maximum(sig_ref[i, k] - base, 0) for i in range(nsig)]
        phi = phi_ref[pl.ds(pl.multiple_of(k * nsig * BLOCK, BLOCK), nsig * BLOCK), :]
        dens = jnp.concatenate(
            [jnp.concatenate([diag_ref[s[i], s[j]] for j in range(nsig)], axis=1) for i in range(nsig)], axis=0
        )
        image = jnp.dot(dens, phi, preferred_element_type=jnp.float32)
        prod = phi.astype(jnp.float32) * image
        total = jnp.sum(prod.reshape(nsig * BLOCK // 8, 8, npts), axis=0)
        return jnp.sum(total, axis=0, keepdims=True)

    def image_step(t, carry):
        first = image_rho(2 * t)
        second = image_rho(2 * t + 1)
        rho_ref[pl.ds(2 * t, 1), :] = first
        rho_ref[pl.ds(2 * t + 1, 1), :] = second
        return carry

    half = slots // 4
    lax.fori_loop(0, half, image_step, 0)

    for j in range(1, nq):
        owner = (me + ncols - j * ratio) % ncols
        pts_copy(j, owner).wait_recv()
        for l in range(1, ratio):
            fan_copy(j, l, owner).start()

    lax.fori_loop(half, slots // 2, image_step, 0)

    slot = lax.broadcasted_iota(jnp.int32, (slots, npts), 0).astype(jnp.float32)
    w = w_ref[...] * jnp.clip(live - slot, 0.0, 1.0)
    rho = jnp.maximum(rho_ref[...], 0.0)
    above = rho > 0.0
    root = jnp.where(above, jnp.exp2(jnp.log2(jnp.where(above, rho, 1.0)) * (1.0 / 3.0)), 0.0)
    energy = jnp.sum(w * -slater * rho * root, axis=1, keepdims=True)
    energy_ref[...] = energy
    pot_all_ref[pl.ds(pl.multiple_of(mine, 8), slots), :] = (w * (-4.0 / 3.0 * slater)) * root
    own_sum = jnp.sum(energy, axis=0, keepdims=True)
    tail = lax.broadcasted_iota(jnp.int32, (8, npts), 0)
    pot_all_ref[pl.ds(pl.multiple_of(mine + slots, 8), 8), :] = jnp.where(
        tail == 0, jnp.broadcast_to(own_sum, (8, npts)), meta_ref[...]
    )

    def pot_slab(which):
        return pot_all_ref.at[pl.ds(pl.multiple_of(which * stride, 8), stride), :]

    def pot_copy(j, owner):
        to = (me + j * ratio) % ncols
        return remote(pot_slab(owner), pot_slab(owner), pot_send.at[j - 1], pot_recv.at[j - 1], group, to)

    def pfan_copy(j, l, owner):
        to = place * ratio + (lane + l) % ratio
        return remote(pot_slab(owner), pot_slab(owner), pfan_send.at[l - 1, j], pfan_recv.at[l - 1, j], group, to)

    for j in range(1, nq):
        pot_copy(j, me).start()
    for l in range(1, ratio):
        pfan_copy(0, l, me).start()

    def settle(c, carry):
        @pl.when(dist(c) < nq - 1)
        def _():
            ring_copy(c).wait_send()

        for j in range(1, ratio):
            sib_copy(c, j, lane).wait_send()
        return carry

    lax.fori_loop(0, chunks, settle, 0)
    for j in range(1, nq):
        pts_copy(j, me).wait_send()
    for l in range(1, ratio):
        sibling = place * ratio + (lane + ratio - l) % ratio
        for j in range(nq):
            fan_copy(j, l, (me + ncols - j * ratio) % ncols).wait_send()
            fan_copy(j, l, (sibling + ncols - j * ratio) % ncols).wait_recv()
    for j in range(1, nq):
        owner = (me + ncols - j * ratio) % ncols
        pot_copy(j, owner).wait_recv()
        for l in range(1, ratio):
            pfan_copy(j, l, owner).start()
    for l in range(1, ratio):
        sibling = place * ratio + (lane + ratio - l) % ratio
        for j in range(nq):
            pfan_copy(j, l, (sibling + ncols - j * ratio) % ncols).wait_recv()

    part_sum = jnp.zeros((8, BLOCK), jnp.float32)
    for d in range(ncols):
        part_sum += pot_all_ref[d * stride + slots : d * stride + slots + 1, 0:BLOCK]
    ebuf_ref[group] = part_sum

    def exc_copy(j, owner):
        return remote(ebuf_ref.at[owner], ebuf_ref.at[owner], exc_send.at[j - 1], exc_recv.at[j - 1], (group + j) % nrows, me)

    for j in range(1, nrows):
        exc_copy(j, group).start()
    for j in range(1, nq):
        pot_copy(j, me).wait_send()
    for l in range(1, ratio):
        for j in range(nq):
            pfan_copy(j, l, (me + ncols - j * ratio) % ncols).wait_send()
    for j in range(1, nrows):
        exc_copy(j, (group + nrows - j) % nrows).wait_recv()
    exc = jnp.zeros((8, BLOCK), jnp.float32)
    for g in range(nrows):
        exc += ebuf_ref[g]
    exc_ref[...] = exc
    for j in range(1, nrows):
        exc_copy(j, group).wait_send()


def strip_kernel(nsig, slots, stride, piece, sig_ref, live_ref, col_ref, pts_ref, wpot_ref, terms_ref, terms_t_ref, out_ref, phi_a, phi_b, scaled_a, scaled_b, list_ref):
    strip = out_ref.shape[0]
    npiece = strip // piece
    start = col_ref[0]
    blocks = [(start + q * piece) // BLOCK for q in range(npiece)]
    out_ref[...] = jnp.zeros_like(out_ref)

    def scan_device(d, n):
        def scan_slot(k, n):
            hit = jnp.bool_(False)
            for i in range(nsig):
                v = sig_ref[(d * nsig + i) * slots + k]
                for block in blocks:
                    hit = hit | (v == block)
            list_ref[n] = d * stride + k
            return n + hit.astype(jnp.int32)

        return lax.fori_loop(0, live_ref[d], scan_slot, n)

    total = lax.fori_loop(0, live_ref.shape[0], scan_device, jnp.int32(0))
    for extra in range(3):
        list_ref[total + extra] = 0

    def blocks_of(row):
        d = row // stride
        return [sig_ref[(d * nsig + i) * slots + row - d * stride] for i in range(nsig)]

    own = terms_ref[pl.ds(pl.multiple_of(start, piece), strip), :]

    def make(index, phi_dst, scaled_dst):
        row = list_ref[index]
        valid = index < total
        feats = point_terms(pts_ref, row)
        s = blocks_of(row)
        terms = jnp.concatenate([terms_t_ref[v] for v in s], axis=1)
        arg = jnp.dot(feats.T.astype(jnp.bfloat16), terms, preferred_element_type=jnp.float32)
        phi_dst[...] = jnp.exp(arg).astype(jnp.bfloat16)
        wpot = wpot_ref[pl.ds(row, 1), :]
        arg = jnp.dot(own, feats.astype(jnp.bfloat16), preferred_element_type=jnp.float32)
        phi = jnp.exp(arg).astype(jnp.bfloat16).astype(jnp.float32)
        for q in range(npiece):
            have = jnp.bool_(False)
            for v in s:
                have = have | (v == blocks[q])
            on = (have & valid).astype(jnp.float32)
            rows = phi[q * piece : (q + 1) * piece] * (wpot * on)
            scaled_dst[pl.ds(q * piece, piece), :] = rows.astype(jnp.bfloat16)

    def add(index, phi_src, scaled_src):
        s = blocks_of(list_ref[index])
        delta = jnp.dot(scaled_src[...], phi_src[...], preferred_element_type=jnp.float32)
        for i in range(nsig):
            cols = pl.ds(pl.multiple_of(s[i] * BLOCK, BLOCK), BLOCK)
            out_ref[:, cols] += delta[:, i * BLOCK : (i + 1) * BLOCK]

    make(0, phi_a, scaled_a)

    def step(t, carry):
        make(2 * t + 1, phi_b, scaled_b)
        add(2 * t, phi_a, scaled_a)
        make(2 * t + 2, phi_a, scaled_a)
        add(2 * t + 1, phi_b, scaled_b)
        return carry

    lax.fori_loop(0, (total + 1) // 2, step, 0)


def shards(density, points, grid_weights, centres, exponents, sig_blocks, live_count):
    nrows = lax.axis_size("rows")
    ncols = lax.axis_size("cols")
    group = lax.axis_index("rows")
    col = lax.axis_index("cols")
    nsig = sig_blocks.shape[1]
    slots, _, npts = points.shape
    own_width = density.shape[0]
    span = own_width // BLOCK
    strip = own_width // ncols
    piece = math.gcd(strip, BLOCK)
    ratio = own_width // density.shape[1]
    nq = ncols // ratio
    stride = slots + 8
    held = span // ratio
    chunks = span * (2 if held % 2 == 0 and slots % (2 * span) == 0 else 1)

    vmem = pl.BlockSpec(memory_space=pltpu.VMEM)
    smem = pl.BlockSpec(memory_space=pltpu.SMEM)
    hbm = pl.BlockSpec(memory_space=pltpu.HBM)

    dma = pltpu.SemaphoreType.DMA
    pts_all, pot_all, energy, exc, terms, terms_t = pl.pallas_call(
        functools.partial(exchange_kernel, nrows, ncols, nsig, chunks, stride),
        out_shape=(
            jax.ShapeDtypeStruct((3, ncols * stride, npts), jnp.float32),
            jax.ShapeDtypeStruct((ncols * stride, npts), jnp.float32),
            jax.ShapeDtypeStruct((slots, 1), jnp.float32),
            jax.ShapeDtypeStruct((8, BLOCK), jnp.float32),
            jax.ShapeDtypeStruct((span, BLOCK, 48), jnp.bfloat16),
            jax.ShapeDtypeStruct((span, 48, BLOCK), jnp.bfloat16),
        ),
        in_specs=[smem, smem, vmem, hbm, vmem, vmem, vmem, vmem],
        out_specs=(vmem,) * 6,
        scratch_shapes=[
            pltpu.VMEM((span, span, BLOCK, BLOCK), jnp.bfloat16),
            pltpu.VMEM((slots * nsig * BLOCK, npts), jnp.bfloat16),
            pltpu.VMEM((slots, npts), jnp.float32),
            pltpu.VMEM((nrows, 8, BLOCK), jnp.float32),
            pltpu.VMEM((8, npts), jnp.float32),
            dma((span // ratio,)),
            dma((chunks,)),
            dma((chunks,)),
            dma((max(ratio - 1, 1), chunks)),
            dma((max(ratio - 1, 1), chunks)),
            dma((max(nq - 1, 1),)),
            dma((max(nq - 1, 1),)),
            dma((max(ratio - 1, 1), nq)),
            dma((max(ratio - 1, 1), nq)),
            dma((max(nq - 1, 1),)),
            dma((max(nq - 1, 1),)),
            dma((max(ratio - 1, 1), nq)),
            dma((max(ratio - 1, 1), nq)),
            dma((max(nrows - 1, 1),)),
            dma((max(nrows - 1, 1),)),
        ],
        compiler_params=pltpu.CompilerParams(
            collective_id=0, has_side_effects=True, vmem_limit_bytes=48 * 1024 * 1024
        ),
        name="exchange",
    )(
        sig_blocks.T, live_count, sig_blocks.T, density.reshape(span, BLOCK, -1), points.transpose(1, 0, 2),
        grid_weights, centres, exponents.reshape(1, -1),
    )
    own_energy = energy.reshape(slots)
    tails = pot_all.reshape(ncols, stride, npts)[:, slots : slots + 8]
    sig_all = (tails[:, 1 : 1 + nsig, :slots].astype(jnp.int32) - group * span).reshape(-1)
    live_all = tails[:, 1 + nsig, 0].astype(jnp.int32)

    xc_strip = pl.pallas_call(
        functools.partial(strip_kernel, nsig, slots, stride, piece),
        out_shape=jax.ShapeDtypeStruct((strip, own_width), jnp.float32),
        in_specs=[smem, smem, smem, vmem, vmem, vmem, vmem],
        out_specs=vmem,
        scratch_shapes=[
            pltpu.VMEM((npts, nsig * BLOCK), jnp.bfloat16),
            pltpu.VMEM((npts, nsig * BLOCK), jnp.bfloat16),
            pltpu.VMEM((strip, npts), jnp.bfloat16),
            pltpu.VMEM((strip, npts), jnp.bfloat16),
            pltpu.SMEM((ncols * slots + 8,), jnp.int32),
        ],
        compiler_params=pltpu.CompilerParams(vmem_limit_bytes=32 * 1024 * 1024),
        name="strip",
    )(sig_all, live_all, (col * strip).reshape(1).astype(jnp.int32), pts_all, pot_all, terms.reshape(own_width, -1), terms_t)
    return (xc_strip.T, own_energy, exc[0, 0])


def solution(mesh):
    placed = (
        P("rows", "cols"),
        P(("rows", "cols"), None, None),
        P(("rows", "cols"), None),
        P(),
        P(),
        P(("rows", "cols"), None),
        P(("rows", "cols")),
    )
    return jax.shard_map(
        shards,
        mesh=mesh,
        in_specs=placed,
        out_specs=(P("rows", "cols"), P(("rows", "cols")), P()),
        check_vma=False,
    )
```

```python
import functools
import math

import jax
import jax.numpy as jnp
from jax import lax
from jax.experimental import pallas as pl
from jax.experimental.pallas import tpu as pltpu
from jax.sharding import PartitionSpec as P

BLOCK = 128
slater = 0.7386


def function_terms(c, a):
    cc = c[0:1] * c[0:1] + c[1:2] * c[1:2] + c[2:3] * c[2:3]
    coef = jnp.concatenate([2.0 * a * c, -a, -a * cc, jnp.zeros_like(c)], axis=0)
    hi = coef.astype(jnp.bfloat16).astype(jnp.float32)
    rest = coef - hi
    mid = rest.astype(jnp.bfloat16).astype(jnp.float32)
    lo = rest - mid
    return jnp.concatenate([hi, mid, lo, hi, mid, hi], axis=0)


def point_terms(pts_ref, row):
    x, y, z = (pts_ref[axis, pl.ds(row, 1), :] for axis in range(3))
    r2 = x * x + y * y + z * z
    one = jnp.ones_like(x)
    zero = jnp.zeros_like(x)
    v = jnp.concatenate([x, y, z, r2, one, zero, zero, zero], axis=0)
    hi = v.astype(jnp.bfloat16).astype(jnp.float32)
    rest = v - hi
    mid = rest.astype(jnp.bfloat16).astype(jnp.float32)
    lo = rest - mid
    return jnp.concatenate([hi, hi, hi, mid, mid, lo], axis=0)


def phi_rows(terms_ref, s, feats):
    terms = jnp.concatenate([terms_ref[v] for v in s], axis=0)
    arg = jnp.dot(terms, feats, preferred_element_type=jnp.float32)
    return jnp.exp(arg).astype(jnp.bfloat16)


def exchange_kernel(
    nrows, ncols, nsig, chunks, stride,
    sig_ref, live_ref, sig_rows_ref, dens_ref, pts_ref, w_ref, centres_ref, expo_ref,
    pts_all_ref, pot_all_ref, energy_ref, exc_ref, terms_ref, terms_t_ref,
    diag_ref, phi_ref, rho_ref, ebuf_ref, meta_ref,
    local_sem, ring_send, ring_recv, sib_send, sib_recv,
    pts_send, pts_recv, fan_send, fan_recv, pot_send, pot_recv, pfan_send, pfan_recv, exc_send, exc_recv,
):
    group = lax.axis_index("rows")
    me = lax.axis_index("cols")
    slots, npts = w_ref.shape
    span = diag_ref.shape[0]
    held = dens_ref.shape[2] // BLOCK
    ratio = span // held
    nq = ncols // ratio
    lane, place = me % ratio, me // ratio

    def ring_of(q):
        return q // 2 * 2 + (q % 2 + q // 2) % 2 if nq % 2 == 0 else q

    direction = 1 - 2 * (lane % 2)
    ring = ring_of(place)
    after = ring_of((ring + direction + nq) % nq)
    dist = ((ring - ring_of(group)) * direction + 2 * nq) % nq

    barrier = pltpu.get_barrier_semaphore()
    for j in range(1, ncols):
        pl.semaphore_signal(
            barrier, inc=1, device_id=(group, (me + j) % ncols), device_id_type=pl.DeviceIdType.MESH
        )
    for j in range(1, nrows):
        pl.semaphore_signal(
            barrier, inc=1, device_id=((group + j) % nrows, me), device_id_type=pl.DeviceIdType.MESH
        )

    base = group * span
    for j in range(span):
        at = pl.ds(pl.multiple_of((base + j) * BLOCK, BLOCK), BLOCK)
        made = function_terms(centres_ref[:, at], expo_ref[:, at])
        terms_t_ref[j] = made.astype(jnp.bfloat16)
        terms_ref[j] = made.T.astype(jnp.bfloat16)
    live = live_ref[0].astype(jnp.float32)
    meta_ref[...] = jnp.zeros_like(meta_ref)
    meta_ref[1 : 1 + nsig, 0:slots] = sig_rows_ref[...].astype(jnp.float32)
    meta_ref[1 + nsig : 2 + nsig, :] = jnp.full((1, npts), live, jnp.float32)

    pl.semaphore_wait(barrier, ncols + nrows - 2)

    def remote(src, dst, send, recv, to_row, to_col):
        return pltpu.make_async_remote_copy(
            src_ref=src, dst_ref=dst, send_sem=send, recv_sem=recv,
            device_id=(to_row, to_col), device_id_type=pl.DeviceIdType.MESH,
        )

    @pl.when(dist == 0)
    def _():
        own = [
            pltpu.make_async_copy(
                dens_ref.at[:, :, pl.ds(j * BLOCK, BLOCK)], diag_ref.at[:, lane * held + j], local_sem.at[j]
            )
            for j in range(held)
        ]
        for copy in own:
            copy.start()
        for copy in own:
            copy.wait()

    cuts = chunks // span
    some = held // cuts

    def part(c, which):
        return diag_ref.at[c // cuts, pl.ds(which * held + c % cuts * some, some)]

    def ring_copy(c):
        return remote(part(c, lane), part(c, lane), ring_send.at[c], ring_recv.at[c], group, after * ratio + lane)

    def sib_copy(c, j, which):
        to = place * ratio + (lane + j) % ratio
        return remote(part(c, which), part(c, which), sib_send.at[j - 1, c], sib_recv.at[j - 1, c], group, to)

    per = slots // chunks
    mine = me * stride
    for axis in range(3):
        pts_all_ref[axis, pl.ds(pl.multiple_of(mine, 8), slots), :] = pts_ref[axis]

    def chunk_step(c, carry):
        @pl.when(dist > 0)
        def _():
            ring_copy(c).wait_recv()

        @pl.when(dist < nq - 1)
        def _():
            ring_copy(c).start()

        for j in range(1, ratio):
            sib_copy(c, j, lane).start()
        for u in range(per):
            k = c * per + u
            feats = point_terms(pts_ref, k).astype(jnp.bfloat16)
            s = [jnp.maximum(sig_ref[i, k] - base, 0) for i in range(nsig)]
            at = pl.multiple_of(k * nsig * BLOCK, nsig * BLOCK)
            phi_ref[pl.ds(at, nsig * BLOCK), :] = phi_rows(terms_ref, s, feats)
        return carry

    lax.fori_loop(0, chunks, chunk_step, 0)

    def slab(which):
        return pts_all_ref.at[:, pl.ds(pl.multiple_of(which * stride, 8), slots), :]

    def pts_copy(j, owner):
        to = (me + j * ratio) % ncols
        return remote(slab(owner), slab(owner), pts_send.at[j - 1], pts_recv.at[j - 1], group, to)

    def fan_copy(j, l, owner):
        to = place * ratio + (lane + l) % ratio
        return remote(slab(owner), slab(owner), fan_send.at[l - 1, j], fan_recv.at[l - 1, j], group, to)

    for j in range(1, nq):
        pts_copy(j, me).start()
    for l in range(1, ratio):
        fan_copy(0, l, me).start()

    def drain(c, carry):
        for j in range(1, ratio):
            sib_copy(c, j, (lane + ratio - j) % ratio).wait_recv()
        return carry

    lax.fori_loop(0, chunks, drain, 0)

    def image_rho(k):
        s = [jnp.maximum(sig_ref[i, k] - base, 0) for i in range(nsig)]
        phi = phi_ref[pl.ds(pl.multiple_of(k * nsig * BLOCK, BLOCK), nsig * BLOCK), :]
        dens = jnp.concatenate(
            [jnp.concatenate([diag_ref[s[i], s[j]] for j in range(nsig)], axis=1) for i in range(nsig)], axis=0
        )
        image = jnp.dot(dens, phi, preferred_element_type=jnp.float32)
        prod = phi.astype(jnp.float32) * image
        total = jnp.sum(prod.reshape(nsig * BLOCK // 8, 8, npts), axis=0)
        return jnp.sum(total, axis=0, keepdims=True)

    def image_step(t, carry):
        first = image_rho(2 * t)
        second = image_rho(2 * t + 1)
        rho_ref[pl.ds(2 * t, 1), :] = first
        rho_ref[pl.ds(2 * t + 1, 1), :] = second
        return carry

    lax.fori_loop(0, slots // 2, image_step, 0)

    for j in range(1, nq):
        owner = (me + ncols - j * ratio) % ncols
        pts_copy(j, owner).wait_recv()
        for l in range(1, ratio):
            fan_copy(j, l, owner).start()


    slot = lax.broadcasted_iota(jnp.int32, (slots, npts), 0).astype(jnp.float32)
    w = w_ref[...] * jnp.clip(live - slot, 0.0, 1.0)
    rho = jnp.maximum(rho_ref[...], 0.0)
    above = rho > 0.0
    root = jnp.where(above, jnp.exp2(jnp.log2(jnp.where(above, rho, 1.0)) * (1.0 / 3.0)), 0.0)
    energy = jnp.sum(w * -slater * rho * root, axis=1, keepdims=True)
    energy_ref[...] = energy
    pot_all_ref[pl.ds(pl.multiple_of(mine, 8), slots), :] = (w * (-4.0 / 3.0 * slater)) * root
    own_sum = jnp.sum(energy, axis=0, keepdims=True)
    tail = lax.broadcasted_iota(jnp.int32, (8, npts), 0)
    pot_all_ref[pl.ds(pl.multiple_of(mine + slots, 8), 8), :] = jnp.where(
        tail == 0, jnp.broadcast_to(own_sum, (8, npts)), meta_ref[...]
    )

    def pot_slab(which):
        return pot_all_ref.at[pl.ds(pl.multiple_of(which * stride, 8), stride), :]

    def pot_copy(j, owner):
        to = (me + j * ratio) % ncols
        return remote(pot_slab(owner), pot_slab(owner), pot_send.at[j - 1], pot_recv.at[j - 1], group, to)

    def pfan_copy(j, l, owner):
        to = place * ratio + (lane + l) % ratio
        return remote(pot_slab(owner), pot_slab(owner), pfan_send.at[l - 1, j], pfan_recv.at[l - 1, j], group, to)

    for j in range(1, nq):
        pot_copy(j, me).start()
    for l in range(1, ratio):
        pfan_copy(0, l, me).start()

    def settle(c, carry):
        @pl.when(dist < nq - 1)
        def _():
            ring_copy(c).wait_send()

        for j in range(1, ratio):
            sib_copy(c, j, lane).wait_send()
        return carry

    lax.fori_loop(0, chunks, settle, 0)
    for j in range(1, nq):
        pts_copy(j, me).wait_send()
    for l in range(1, ratio):
        sibling = place * ratio + (lane + ratio - l) % ratio
        for j in range(nq):
            fan_copy(j, l, (me + ncols - j * ratio) % ncols).wait_send()
            fan_copy(j, l, (sibling + ncols - j * ratio) % ncols).wait_recv()
    for j in range(1, nq):
        owner = (me + ncols - j * ratio) % ncols
        pot_copy(j, owner).wait_recv()
        for l in range(1, ratio):
            pfan_copy(j, l, owner).start()
    for l in range(1, ratio):
        sibling = place * ratio + (lane + ratio - l) % ratio
        for j in range(nq):
            pfan_copy(j, l, (sibling + ncols - j * ratio) % ncols).wait_recv()

    part_sum = jnp.zeros((8, BLOCK), jnp.float32)
    for d in range(ncols):
        part_sum += pot_all_ref[d * stride + slots : d * stride + slots + 1, 0:BLOCK]
    ebuf_ref[group] = part_sum

    def exc_copy(j, owner):
        return remote(ebuf_ref.at[owner], ebuf_ref.at[owner], exc_send.at[j - 1], exc_recv.at[j - 1], (group + j) % nrows, me)

    for j in range(1, nrows):
        exc_copy(j, group).start()
    for j in range(1, nq):
        pot_copy(j, me).wait_send()
    for l in range(1, ratio):
        for j in range(nq):
            pfan_copy(j, l, (me + ncols - j * ratio) % ncols).wait_send()
    for j in range(1, nrows):
        exc_copy(j, (group + nrows - j) % nrows).wait_recv()
    exc = jnp.zeros((8, BLOCK), jnp.float32)
    for g in range(nrows):
        exc += ebuf_ref[g]
    exc_ref[...] = exc
    for j in range(1, nrows):
        exc_copy(j, group).wait_send()


def strip_kernel(nsig, slots, stride, piece, sig_ref, live_ref, col_ref, pts_ref, wpot_ref, terms_ref, terms_t_ref, out_ref, phi_a, phi_b, scaled_a, scaled_b, list_ref):
    strip = out_ref.shape[0]
    npiece = strip // piece
    start = col_ref[0]
    blocks = [(start + q * piece) // BLOCK for q in range(npiece)]
    out_ref[...] = jnp.zeros_like(out_ref)

    def scan_device(d, n):
        def scan_slot(k, n):
            hit = jnp.bool_(False)
            for i in range(nsig):
                v = sig_ref[(d * nsig + i) * slots + k]
                for block in blocks:
                    hit = hit | (v == block)
            list_ref[n] = d * stride + k
            return n + hit.astype(jnp.int32)

        return lax.fori_loop(0, live_ref[d], scan_slot, n)

    total = lax.fori_loop(0, live_ref.shape[0], scan_device, jnp.int32(0))
    for extra in range(3):
        list_ref[total + extra] = 0

    def blocks_of(row):
        d = row // stride
        return [sig_ref[(d * nsig + i) * slots + row - d * stride] for i in range(nsig)]

    own = terms_ref[pl.ds(pl.multiple_of(start, piece), strip), :]

    def make(index, phi_dst, scaled_dst):
        row = list_ref[index]
        valid = index < total
        feats = point_terms(pts_ref, row)
        s = blocks_of(row)
        terms = jnp.concatenate([terms_t_ref[v] for v in s], axis=1)
        arg = jnp.dot(feats.T.astype(jnp.bfloat16), terms, preferred_element_type=jnp.float32)
        phi_dst[...] = jnp.exp(arg).astype(jnp.bfloat16)
        wpot = wpot_ref[pl.ds(row, 1), :]
        arg = jnp.dot(own, feats.astype(jnp.bfloat16), preferred_element_type=jnp.float32)
        phi = jnp.exp(arg).astype(jnp.bfloat16).astype(jnp.float32)
        for q in range(npiece):
            have = jnp.bool_(False)
            for v in s:
                have = have | (v == blocks[q])
            on = (have & valid).astype(jnp.float32)
            rows = phi[q * piece : (q + 1) * piece] * (wpot * on)
            scaled_dst[pl.ds(q * piece, piece), :] = rows.astype(jnp.bfloat16)

    def add(index, phi_src, scaled_src):
        s = blocks_of(list_ref[index])
        delta = jnp.dot(scaled_src[...], phi_src[...], preferred_element_type=jnp.float32)
        for i in range(nsig):
            cols = pl.ds(pl.multiple_of(s[i] * BLOCK, BLOCK), BLOCK)
            out_ref[:, cols] += delta[:, i * BLOCK : (i + 1) * BLOCK]

    make(0, phi_a, scaled_a)

    def step(t, carry):
        make(2 * t + 1, phi_b, scaled_b)
        add(2 * t, phi_a, scaled_a)
        make(2 * t + 2, phi_a, scaled_a)
        add(2 * t + 1, phi_b, scaled_b)
        return carry

    lax.fori_loop(0, (total + 1) // 2, step, 0)


def shards(density, points, grid_weights, centres, exponents, sig_blocks, live_count):
    nrows = lax.axis_size("rows")
    ncols = lax.axis_size("cols")
    group = lax.axis_index("rows")
    col = lax.axis_index("cols")
    nsig = sig_blocks.shape[1]
    slots, _, npts = points.shape
    own_width = density.shape[0]
    span = own_width // BLOCK
    strip = own_width // ncols
    piece = math.gcd(strip, BLOCK)
    ratio = own_width // density.shape[1]
    nq = ncols // ratio
    stride = slots + 8
    held = span // ratio
    chunks = span * (2 if held % 2 == 0 and slots % (2 * span) == 0 else 1)

    vmem = pl.BlockSpec(memory_space=pltpu.VMEM)
    smem = pl.BlockSpec(memory_space=pltpu.SMEM)
    hbm = pl.BlockSpec(memory_space=pltpu.HBM)

    dma = pltpu.SemaphoreType.DMA
    pts_all, pot_all, energy, exc, terms, terms_t = pl.pallas_call(
        functools.partial(exchange_kernel, nrows, ncols, nsig, chunks, stride),
        out_shape=(
            jax.ShapeDtypeStruct((3, ncols * stride, npts), jnp.float32),
            jax.ShapeDtypeStruct((ncols * stride, npts), jnp.float32),
            jax.ShapeDtypeStruct((slots, 1), jnp.float32),
            jax.ShapeDtypeStruct((8, BLOCK), jnp.float32),
            jax.ShapeDtypeStruct((span, BLOCK, 48), jnp.bfloat16),
            jax.ShapeDtypeStruct((span, 48, BLOCK), jnp.bfloat16),
        ),
        in_specs=[smem, smem, vmem, hbm, vmem, vmem, vmem, vmem],
        out_specs=(vmem,) * 6,
        scratch_shapes=[
            pltpu.VMEM((span, span, BLOCK, BLOCK), jnp.bfloat16),
            pltpu.VMEM((slots * nsig * BLOCK, npts), jnp.bfloat16),
            pltpu.VMEM((slots, npts), jnp.float32),
            pltpu.VMEM((nrows, 8, BLOCK), jnp.float32),
            pltpu.VMEM((8, npts), jnp.float32),
            dma((span // ratio,)),
            dma((chunks,)),
            dma((chunks,)),
            dma((max(ratio - 1, 1), chunks)),
            dma((max(ratio - 1, 1), chunks)),
            dma((max(nq - 1, 1),)),
            dma((max(nq - 1, 1),)),
            dma((max(ratio - 1, 1), nq)),
            dma((max(ratio - 1, 1), nq)),
            dma((max(nq - 1, 1),)),
            dma((max(nq - 1, 1),)),
            dma((max(ratio - 1, 1), nq)),
            dma((max(ratio - 1, 1), nq)),
            dma((max(nrows - 1, 1),)),
            dma((max(nrows - 1, 1),)),
        ],
        compiler_params=pltpu.CompilerParams(
            collective_id=0, has_side_effects=True, vmem_limit_bytes=48 * 1024 * 1024
        ),
        name="exchange",
    )(
        sig_blocks.T, live_count, sig_blocks.T, density.reshape(span, BLOCK, -1), points.transpose(1, 0, 2),
        grid_weights, centres, exponents.reshape(1, -1),
    )
    own_energy = energy.reshape(slots)
    tails = pot_all.reshape(ncols, stride, npts)[:, slots : slots + 8]
    sig_all = (tails[:, 1 : 1 + nsig, :slots].astype(jnp.int32) - group * span).reshape(-1)
    live_all = tails[:, 1 + nsig, 0].astype(jnp.int32)

    xc_strip = pl.pallas_call(
        functools.partial(strip_kernel, nsig, slots, stride, piece),
        out_shape=jax.ShapeDtypeStruct((strip, own_width), jnp.float32),
        in_specs=[smem, smem, smem, vmem, vmem, vmem, vmem],
        out_specs=vmem,
        scratch_shapes=[
            pltpu.VMEM((npts, nsig * BLOCK), jnp.bfloat16),
            pltpu.VMEM((npts, nsig * BLOCK), jnp.bfloat16),
            pltpu.VMEM((strip, npts), jnp.bfloat16),
            pltpu.VMEM((strip, npts), jnp.bfloat16),
            pltpu.SMEM((ncols * slots + 8,), jnp.int32),
        ],
        compiler_params=pltpu.CompilerParams(vmem_limit_bytes=32 * 1024 * 1024),
        name="strip",
    )(sig_all, live_all, (col * strip).reshape(1).astype(jnp.int32), pts_all, pot_all, terms.reshape(own_width, -1), terms_t)
    return (xc_strip.T, own_energy, exc[0, 0])


def solution(mesh):
    placed = (
        P("rows", "cols"),
        P(("rows", "cols"), None, None),
        P(("rows", "cols"), None),
        P(),
        P(),
        P(("rows", "cols"), None),
        P(("rows", "cols")),
    )
    return jax.shard_map(
        shards,
        mesh=mesh,
        in_specs=placed,
        out_specs=(P("rows", "cols"), P(("rows", "cols")), P()),
        check_vma=False,
    )
```
